256 devices in a mesh: ctx: 16 (over x, y_lo, core), exp: 16 (over z, y_hi).
Axes of the slice: x: 4, y: 4 (y_hi: 2, y_lo: 2; y = y_hi * 2 + y_lo), z: 8, core: 2. Of those that a mesh axis runs over, the one named last changes fastest.
Arguments:
- queries: bfloat16 [2048, 6144], P('ctx', 'exp'), may hold values from -8 to 8
- keys: bfloat16 [2048, 1024], P('ctx'), may hold values from -8 to 8
- values: bfloat16 [2048, 1024], P('ctx'), may hold values from -6 to 6
- segment_ids: int32 [2048], P('ctx'), may hold values from 0 to 1, never falling along the last dimension, each value on 1 to 1536 neighbouring positions
- residual: bfloat16 [2048, 6144], P(('ctx', 'exp')), may hold values from -6 to 6
- w_out: bfloat16 [6144, 6144], P('exp', 'ctx'), may hold values from -0.078125 to 0.078125
- norm_gain: float32 [6144], replicated, may hold values from 0.25 to 1.75
- w_router: bfloat16 [6144, 8], replicated, may hold values from -0.078125 to 0.078125
- routes: int32 [2048, 2], P(('ctx', 'exp')), may hold values from 0 to 7, all different within a row; in each aligned block of 8 rows (0 to 7, 8 to 15, ...) at most 3 rows name the same one
- w_gate: bfloat16 [16, 6144, 4096], P('exp', None, 'ctx'), may hold values from -0.078125 to 0.078125
- w_up: bfloat16 [16, 6144, 4096], P('exp', None, 'ctx'), may hold values from -0.078125 to 0.078125
- w_down: bfloat16 [16, 4096, 6144], P('exp', 'ctx'), may hold values from -0.0625 to 0.0625
Outputs:
- layer_out: bfloat16 [2048, 6144], P(('ctx', 'exp'))
The draws below stay inside these ranges and needn't reach their ends.
Inputs may be any that keep to these rules, and one draw needn't show every extreme that they name: `routes`: in each aligned block of 8 tokens (one device's tokens) no expert is named more than 3 times; some block names one exactly 3 times. A token's two entries differ. `segment_ids`: never falling: the first 512 to 1536 positions are 0, the rest 1.
All inputs are finite; a program needn't handle non-finite values.
Results may differ from the reference program's by a relative error of at most 0.02.
Values may be sent and summed in bfloat16 or wider, within the bound.
No kernel may reach another device: no remote copies, remote signals or barrier semaphores. Data moves between devices by JAX's collectives and lax.ppermute only.
A program may use at most 128 MiB of HBM per device.

```python
import math
import jax
import jax.numpy as jnp
import numpy as np
from jax import lax

D = 6144
HEADS = 48
KVH = 8
HD = 128
EXPERTS = 8
FFW = 8192
TOKENS = 2048
TOKE = 8
QHD = 3
LC = 256
CAP = 3
SEGMOST = 1536
N_EXP = 16


def attention_pair(key):
    base_key = jax.random.fold_in(key, 4242)
    query_key, keys_key = jax.random.split(base_key, 2)
    query_draw = jnp.clip(jax.random.normal(query_key, (TOKENS, HEADS * HD), jnp.float32) * 2.0, -8.0, 8.0)
    key_draw = jnp.clip(jax.random.normal(keys_key, (TOKENS, KVH * HD), jnp.float32) * 1.5, -8.0, 8.0)
    return (query_draw, key_draw)


def draw_queries(key, part):
    return attention_pair(key)[0].astype(jnp.bfloat16)


def draw_keys(key, part):
    return attention_pair(key)[1].astype(jnp.bfloat16)


def levels(own_key, extent, cuts, least, top_value):
    def one(dim, blocks):
        steps = jax.random.uniform(jax.random.fold_in(jax.random.fold_in(own_key, 6), dim), (blocks,), jnp.float32, least / len(cuts), top_value / len(cuts))
        return jnp.repeat(jnp.exp(steps), extent[dim] // blocks).reshape((-1,) + (1,) * (len(extent) - dim - 1))

    level = one(*cuts[0])
    for cut in cuts[1:]:
        level = level * one(*cut)
    return level


def profile(number_of, total, most, lean):
    portions = [(1 << 20) // math.isqrt(standing ** lean) + 1 for standing in range(2, number_of + 1)]
    surplus, given = total - most - (number_of - 1), [1] * (number_of - 1)
    while surplus > 0:
        free = [i for i in range(number_of - 1) if given[i] < most]
        mass, left = sum([portions[i] for i in free]), surplus
        for i in free:
            addition = min(most - given[i], max(1, left * portions[i] // mass), surplus)
            given[i] = given[i] + addition
            surplus = surplus - addition
    return np.array([most] + given)


def uneven_parts(rng, amount, total, bound, slope):
    if amount == 2:
        one = jax.random.randint(rng, (), max(1, total - bound), min(bound, total - 1) + 1)
        return jnp.stack([one, total - one])
    lengths = jnp.asarray(profile(amount, total, bound, slope), jnp.int32)
    twos = (amount - 1) // 2
    donor, receiver = lengths[1:1 + 2 * twos:2], lengths[2:2 + 2 * twos:2]
    room = jnp.minimum(donor - 1, bound - receiver)
    passed = jax.random.randint(jax.random.fold_in(rng, 1), (twos,), 0, 1 << 20) % (room + 1)
    lengths = lengths.at[1:1 + 2 * twos:2].set(donor - passed).at[2:2 + 2 * twos:2].set(receiver + passed)
    return lengths[jax.random.permutation(jax.random.fold_in(rng, 2), amount)]


def shared_out(key, own, number, rows, count, top, bound, slope):
    ranking = jax.random.permutation(key, count)
    crowded, usual = load_shares(count, rows * top, bound, slope, True), load_shares(count, rows * top, bound, slope, False)
    places = jnp.arange(count)

    def named(sizes, offset_by):
        used = int((sizes > 0).sum())
        fixed = max(1, used // 4)
        moved = fixed + (places - fixed + offset_by * (used - fixed)) % max(1, count - fixed)
        return jnp.zeros((count,), jnp.int32).at[ranking[jnp.where(places < fixed, places, moved)]].set(jnp.asarray(sizes, jnp.int32))

    sizes = jnp.where(number % 4 == 0, named(crowded, number // 4), named(usual, number - number // 4 - 1))
    mixed = jax.random.permutation(jax.random.fold_in(own, 3), count)
    donor, sink = mixed[0:count // 2 * 2:2], mixed[1:count // 2 * 2:2]
    slack = jnp.minimum(sizes[donor] - 1, bound - sizes[sink]) // 2
    slack = jnp.where((donor == ranking[0]) | (sink == ranking[0]) | (sizes[sink] == 0), 0, jnp.maximum(slack, 0))
    moved = jax.random.randint(jax.random.fold_in(own, 4), (count // 2,), 0, 1 << 20) % (slack + 1)
    sizes = sizes.at[donor].add(-moved).at[sink].add(moved)
    items = jnp.searchsorted(jnp.cumsum(sizes), jnp.arange(rows * top), side="right").astype(jnp.int32)
    grid = items.reshape(top, rows).T
    grid = grid[jax.random.permutation(jax.random.fold_in(own, 1), rows)]
    offset_by = jax.random.randint(jax.random.fold_in(own, 2), (rows, 1), 0, top)
    return jnp.take_along_axis(grid, (jnp.arange(top)[None, :] + offset_by) % top, axis=1)


def load_shares(number_of, total, limit, slope, full):
    loads = [(1 << 20) // math.isqrt(rank ** slope) + 1 for rank in range(1, number_of + 1)]
    largest = limit if full else min(limit, max(-(-total // number_of), total * loads[0] // sum(loads)))
    least = 1 if total - largest >= number_of - 1 else 0
    given, spare = [largest] + [least] * (number_of - 1), total - largest - least * (number_of - 1)
    while spare > 0:
        movable = [i for i in range(1, number_of) if given[i] < largest] or [i for i in range(1, number_of) if given[i] < limit]
        mass, left = sum([loads[i] for i in movable]), spare
        for i in movable:
            extra = min(limit - given[i], max(1, left * loads[i] // mass), spare)
            given[i] = given[i] + extra
            spare = spare - extra
    return np.array(given)


def bell_draw(stream_key, shape, scale, reach, shards=(), held_as=jnp.bfloat16):
    entries = jax.random.normal(stream_key, shape, jnp.float32) * scale
    if len(shards) > 0:
        entries = levels(stream_key, shape, shards, -0.22, 0.18) * entries
    return jnp.clip(entries, min=-reach, max=reach).astype(held_as)


def setup_inputs(seed: int = 0) -> dict:
    key_list = jax.random.split(jax.random.key(seed), 13)
    queries = draw_queries(jax.random.fold_in(key_list[12], 71), 0)
    keys = draw_keys(jax.random.fold_in(key_list[12], 71), 0)
    values = bell_draw(key_list[2], (TOKENS, KVH * HD), 1.0, 6.0, ((0, 16),))
    segment_ids = jnp.searchsorted(jnp.cumsum(uneven_parts(key_list[3], 2, TOKENS, SEGMOST, 0)), jnp.arange(TOKENS), side="right").astype(jnp.int32)
    residual = bell_draw(key_list[4], (TOKENS, D), 1.0, 6.0, ((0, 256),))
    w_out = bell_draw(key_list[5], (HEADS * HD, D), (HEADS * HD) ** -0.5, 0.078125, ((0, 16), (1, 16)))
    norm_gain = jnp.clip(1.0 + 0.15 * jax.random.normal(key_list[6], (D,), jnp.float32), 0.25, 1.75)
    w_router = bell_draw(key_list[7], (D, EXPERTS), D ** -0.5, 0.078125)
    routes_keys = jax.random.split(jax.random.fold_in(key_list[8], 1), TOKENS // TOKE)
    routes_turns = jax.random.permutation(jax.random.fold_in(key_list[8], 3), TOKENS // TOKE)
    routes = jax.vmap(lambda own, number: shared_out(jax.random.fold_in(key_list[8], 2), own, number, TOKE, EXPERTS, 2, CAP, 1))(routes_keys, routes_turns).reshape((TOKENS, 2))
    w_gate = bell_draw(key_list[9], (N_EXP, D, EXPERTS * FFW // N_EXP), D ** -0.5, 0.078125, ((0, 16), (2, 16)))
    w_up = bell_draw(key_list[10], (N_EXP, D, EXPERTS * FFW // N_EXP), D ** -0.5, 0.078125, ((0, 16), (2, 16)))
    w_down = bell_draw(key_list[11], (N_EXP, EXPERTS * FFW // N_EXP, D), FFW ** -0.5, 0.0625, ((0, 16), (1, 16)))
    return {"queries": queries, "keys": keys, "values": values, "segment_ids": segment_ids, "residual": residual, "w_out": w_out, "norm_gain": norm_gain, "w_router": w_router, "routes": routes, "w_gate": w_gate, "w_up": w_up, "w_down": w_down}


NEG_FILL = -1e+30
EPSILON = 1e-05

def attend_group(query_group, key_head, value_head, allowed):
    scores = jnp.einsum('gqd,kd->gqk', query_group.astype(jnp.float32), key_head.astype(jnp.float32)) * HD ** (-0.5)
    scores = jnp.where(allowed[None], scores, NEG_FILL)
    peak = lax.optimization_barrier(jnp.max(scores, axis=-1, keepdims=True))
    weights = jnp.where(allowed[None], jnp.exp(scores - peak), 0.0)
    total = lax.optimization_barrier(jnp.sum(weights, axis=-1, keepdims=True))
    weights_half = lax.optimization_barrier(weights.astype(jnp.bfloat16))
    summed = jnp.einsum('gqk,kd->gqd', weights_half.astype(jnp.float32), value_head.astype(jnp.float32))
    return (summed / total).astype(jnp.bfloat16)

def reference(queries, keys, values, segment_ids, residual, w_out, norm_gain, w_router, routes, w_gate, w_up, w_down):
    group_size = HEADS // KVH
    position = jnp.arange(TOKENS, dtype=jnp.int32)
    allowed = (position[None, :] <= position[:, None]) & (segment_ids[None, :] == segment_ids[:, None])
    query_heads = queries.reshape(TOKENS, KVH, group_size, HD).transpose(1, 2, 0, 3)
    key_heads = keys.reshape(TOKENS, KVH, HD).transpose(1, 0, 2)
    value_heads = values.reshape(TOKENS, KVH, HD).transpose(1, 0, 2)
    attended = lax.map(lambda item: attend_group(item[0], item[1], item[2], allowed), (query_heads, key_heads, value_heads))
    attention = attended.transpose(2, 0, 1, 3).reshape(TOKENS, HEADS * HD)
    head_width = QHD * HD
    mixed_sum = jnp.zeros((TOKENS, D), jnp.float32)
    for head_block in range(N_EXP):
        head_term = jnp.dot(attention[:, head_block * head_width:(head_block + 1) * head_width], w_out[head_block * head_width:(head_block + 1) * head_width], preferred_element_type=jnp.float32).astype(jnp.bfloat16)
        head_term = lax.optimization_barrier(head_term)
        mixed_sum = mixed_sum + head_term.astype(jnp.float32)
    mixed = residual.astype(jnp.float32) + mixed_sum
    normed = (mixed * lax.rsqrt(lax.optimization_barrier(jnp.mean(mixed * mixed, axis=-1, keepdims=True)) + EPSILON) * norm_gain).astype(jnp.bfloat16)
    logits = jnp.dot(normed, w_router, preferred_element_type=jnp.float32)
    chosen = jnp.take_along_axis(logits, routes, axis=1)
    gates = jax.nn.softmax(chosen, axis=-1)
    block_count = TOKENS // TOKE
    route_expert = routes.reshape(-1)
    expert_ids = jnp.arange(EXPERTS, dtype=jnp.int32)
    onehot = (route_expert.reshape(block_count, 2 * TOKE)[..., None] == expert_ids).astype(jnp.int32)
    ranks = lax.optimization_barrier(jnp.sum((jnp.cumsum(onehot, axis=1) - onehot) * onehot, axis=-1)).reshape(-1)
    route_ids = jnp.arange(2 * TOKENS, dtype=jnp.int32)
    source_block = route_ids // (2 * TOKE)
    table = jnp.full((EXPERTS, block_count, CAP), 2 * TOKENS, jnp.int32).at[route_expert, source_block, ranks].set(route_ids)
    slot_routes = table.reshape(EXPERTS, block_count * CAP)
    normed_routes = jnp.concatenate([jnp.repeat(normed, 2, axis=0), jnp.zeros((1, D), jnp.bfloat16)], axis=0)
    piece_cols = EXPERTS * FFW // N_EXP
    zero_index = jnp.zeros((), jnp.int32)

    def expert_out(item):
        rows_expert, expert_index = item

        def add_slice(total_out, slice_index):
            start_col = (expert_index * FFW + slice_index * LC).astype(jnp.int32)
            piece_index = (start_col // piece_cols).astype(jnp.int32)
            offset = (start_col % piece_cols).astype(jnp.int32)
            gate_slice = lax.dynamic_slice(w_gate, (piece_index, zero_index, offset), (1, D, LC))[0]
            up_slice = lax.dynamic_slice(w_up, (piece_index, zero_index, offset), (1, D, LC))[0]
            down_slice = lax.dynamic_slice(w_down, (piece_index, offset, zero_index), (1, LC, D))[0]
            gate_val = jnp.dot(rows_expert, gate_slice, preferred_element_type=jnp.float32)
            up_val = jnp.dot(rows_expert, up_slice, preferred_element_type=jnp.float32)
            activated = (jax.nn.silu(gate_val) * up_val).astype(jnp.bfloat16)
            slice_out = jnp.dot(activated, down_slice, preferred_element_type=jnp.float32).astype(jnp.bfloat16)
            slice_out = lax.optimization_barrier(slice_out)
            return (total_out + slice_out.astype(jnp.float32), None)
        start_total = jnp.zeros((block_count * CAP, D), jnp.float32)
        final_total, unused = lax.scan(add_slice, start_total, jnp.arange(FFW // LC, dtype=jnp.int32))
        return final_total
    rows_all = normed_routes[slot_routes]
    slot_out = lax.map(expert_out, (rows_all, expert_ids))
    route_out = jnp.zeros((2 * TOKENS + 1, D), jnp.float32).at[slot_routes.reshape(-1)].add(slot_out.reshape(-1, D))[:2 * TOKENS]
    mixture = lax.optimization_barrier(jnp.sum(gates[..., None] * route_out.reshape(TOKENS, 2, D), axis=1))
    return (mixed + mixture).astype(jnp.bfloat16)
```

```python
import jax
import jax.numpy as jnp
import numpy as np
from jax import lax
from jax.sharding import Mesh, PartitionSpec as P

HEADS = 48
KVH = 8
HD = 128
EXPERTS = 8
NEG_FILL = -1e30
EPSILON = 1e-05
SLOTS = 3

X, CTX, EXP, Y = "x", ("x", "yl", "core"), ("z", "yh"), ("yl", "yh")
BF, F32 = jnp.bfloat16, jnp.float32


def y_place(y):
    return y % 2 * 2 + y // 2


def shift(value, axis, by):
    if axis == Y:
        pairs = [(y_place(i), y_place((i + by) % 4)) for i in range(4)]
    else:
        pairs = [(i, (i + by) % 4) for i in range(4)]
    return lax.ppermute(value, axis, pairs)


def swap(value, axis):
    return lax.ppermute(value, axis, [(0, 1), (1, 0)])


def from_three(value, axis):
    return [shift(value, axis, 1), shift(value, axis, -1), shift(value, axis, 2)]


def to_three(blocks, axis):
    return [shift(blocks[1], axis, -1), shift(blocks[2], axis, 1), shift(blocks[3], axis, 2)]


def total(first, *others):
    result = first.astype(F32)
    for other in others:
        result = result + other.astype(F32)
    return result


def attend(queries, keys, values, segment_ids):
    z = lax.axis_index("z")
    rows = queries.shape[0]
    seg_row = jnp.pad(segment_ids.astype(BF)[None, :], ((0, 7), (0, rows)))
    block = jnp.concatenate(
        [
            jnp.concatenate(
                [
                    lax.dynamic_slice_in_dim(keys, z * HD, HD, 1),
                    lax.dynamic_slice_in_dim(values, z * HD, HD, 1),
                ],
                axis=1,
            ),
            seg_row,
        ],
        axis=0,
    )
    x, yl, core = lax.axis_index("x"), lax.axis_index("yl"), lax.axis_index("core")
    blocks = jnp.stack([block] + from_three(block, X))
    blocks = jnp.stack([blocks, swap(blocks, "yl")])
    blocks = jnp.stack([blocks, swap(blocks, "core")])
    places = [
        ((x + dx) % 4) * 4 + ((yl + dy) % 2) * 2 + (core + dc) % 2
        for dc in (0, 1)
        for dy in (0, 1)
        for dx in (0, 3, 1, 2)
    ]
    blocks = blocks.reshape(16, rows + 8, 2 * HD)
    key_rows = blocks[:, :rows, :HD].reshape(16 * rows, HD)
    value_rows = blocks[:, :rows, HD:].reshape(16 * rows, HD)
    seg_keys = blocks[:, rows, :rows].reshape(16 * rows).astype(jnp.int32)
    row_ids = jnp.arange(rows, dtype=jnp.int32)
    key_pos = (jnp.stack(places)[:, None] * rows + row_ids[None, :]).reshape(16 * rows)
    query_pos = (x * 4 + yl * 2 + core) * rows + row_ids
    allowed = (key_pos[None, :] <= query_pos[:, None]) & (
        seg_keys[None, :] == segment_ids[:, None]
    )
    head_count = queries.shape[1] // HD
    query_heads = queries.reshape(rows, head_count, HD)
    scores = jnp.einsum("qrd,kd->rqk", query_heads, key_rows, preferred_element_type=F32)
    scores = jnp.where(allowed[None], scores * HD ** (-0.5), NEG_FILL)
    peak = jnp.max(scores, axis=-1, keepdims=True)
    weights = jnp.where(allowed[None], jnp.exp(scores - peak), 0.0)
    sums = jnp.sum(weights, axis=-1)
    update = jnp.einsum(
        "rqk,kd->rqd", weights.astype(BF), value_rows, preferred_element_type=F32
    )
    attention = (update / sums[..., None]).astype(BF)
    return attention.transpose(1, 0, 2).reshape(rows, head_count * HD)


def gather_plane(rows):
    half = rows.shape[0] // 2
    first, second = rows[:half], rows[half:]
    first = jnp.concatenate([first] + from_three(first, X))
    second = jnp.concatenate([second] + from_three(second, Y))
    first = jnp.concatenate([first] + from_three(first, Y))
    second = jnp.concatenate([second] + from_three(second, X))
    return first, second


def scatter_plane(first, second):
    width = first.shape[-1]
    first = first.reshape(4, -1, width)
    second = second.reshape(4, -1, width)
    first_in, second_in = to_three(first, Y), to_three(second, X)
    first = total(first[0], *first_in).astype(BF).reshape(4, -1, width)
    second = total(second[0], *second_in).astype(BF).reshape(4, -1, width)
    first_in, second_in = to_three(first, X), to_three(second, Y)
    return jnp.concatenate(
        [total(first[0], *first_in).astype(BF), total(second[0], *second_in).astype(BF)]
    )


def shards(
    queries,
    keys,
    values,
    segment_ids,
    residual,
    w_out,
    norm_gain,
    w_router,
    routes,
    w_gate,
    w_up,
    w_down,
):
    w_out_all = lax.all_gather(w_out, CTX, axis=1, tiled=True)
    attention = attend(queries, keys, values, segment_ids)
    head_partial = jnp.dot(attention, w_out_all, preferred_element_type=F32).astype(BF)
    width = head_partial.shape[1]
    tokens = routes.shape[0]
    head_terms = lax.all_to_all(
        head_partial.reshape(16, tokens, width), EXP, split_axis=0, concat_axis=0, tiled=True
    )
    mixed = residual.astype(F32) + jnp.sum(head_terms.astype(F32), axis=0)
    normed = (
        mixed * lax.rsqrt(jnp.mean(mixed * mixed, axis=-1, keepdims=True) + EPSILON) * norm_gain
    ).astype(BF)

    route_flat = routes.reshape(-1)
    expert_ids = jnp.arange(EXPERTS, dtype=jnp.int32)
    onehot = (route_flat[:, None] == expert_ids).astype(jnp.int32)
    ranks = jnp.sum((jnp.cumsum(onehot, axis=0) - onehot) * onehot, axis=-1)
    slot_of_route = (route_flat * SLOTS + ranks).reshape(tokens, 2)
    slot_ids = jnp.arange(EXPERTS * SLOTS, dtype=jnp.int32)
    hot = slot_of_route[:, :, None] == slot_ids
    picks = jnp.any(hot, axis=1).astype(BF)
    outgoing = jnp.dot(picks.T, normed, preferred_element_type=F32).astype(BF)

    incoming = lax.all_to_all(
        outgoing.reshape(EXPERTS, SLOTS, width), "z", split_axis=0, concat_axis=0, tiled=True
    ).reshape(EXPERTS * SLOTS, width)
    first, second = gather_plane(incoming)
    other_first, other_second = swap(first, "core"), swap(second, "core")
    gate_weight, up_weight, down_weight = w_gate[0], w_up[0], w_down[0]

    def expert(rows):
        gate_val = jnp.dot(rows, gate_weight, preferred_element_type=F32)
        up_val = jnp.dot(rows, up_weight, preferred_element_type=F32)
        hidden = (jax.nn.silu(gate_val) * up_val).astype(BF)
        return jnp.dot(hidden, down_weight, preferred_element_type=F32).astype(BF)

    own = expert(jnp.concatenate([first, second]))
    other = expert(jnp.concatenate([other_first, other_second]))
    half = first.shape[0]
    first = total(own[:half], swap(other[:half], "core")).astype(BF)
    second = total(own[half:], swap(other[half:], "core")).astype(BF)
    slot_sums = scatter_plane(first, second)
    returned = lax.all_to_all(
        slot_sums.reshape(EXPERTS, SLOTS, width), "z", split_axis=0, concat_axis=0, tiled=True
    ).reshape(EXPERTS * SLOTS, width)

    logits = jnp.dot(normed, w_router, preferred_element_type=F32)
    chosen = jnp.sum((routes[..., None] == expert_ids).astype(F32) * logits[:, None, :], axis=-1)
    gates = jax.nn.softmax(chosen, axis=-1)
    slot_gates = jnp.sum(jnp.where(hot, gates[:, :, None], 0.0), axis=1)
    mixture = jnp.dot(
        slot_gates,
        returned.astype(F32),
        precision=lax.Precision.HIGHEST,
        preferred_element_type=F32,
    )
    return (mixed + mixture).astype(BF)


def solution(mesh):
    fine = Mesh(mesh.devices.reshape(4, 2, 2, 8, 2), ("x", "yl", "core", "z", "yh"))
    both = CTX + EXP
    placed = (
        P(CTX, EXP),
        P(CTX, None),
        P(CTX, None),
        P(CTX),
        P(both, None),
        P(EXP, CTX),
        P(),
        P(),
        P(both, None),
        P(EXP, None, CTX),
        P(EXP, None, CTX),
        P(EXP, CTX, None),
    )
    return jax.shard_map(
        shards, mesh=fine, in_specs=placed, out_specs=P(both, None), check_vma=False
    )
```

```python
import jax
import jax.numpy as jnp
import numpy as np
from jax import lax
from jax.experimental import pallas as pl
from jax.experimental.pallas import tpu as pltpu
from jax.sharding import Mesh, PartitionSpec as P

HEADS = 48
KVH = 8
HD = 128
EXPERTS = 8
NEG_FILL = -1e30
EPSILON = 1e-05
SLOTS = 3

X, CTX, EXP, Y = "x", ("x", "yl", "core"), ("z", "yh"), ("yl", "yh")
BF, F32 = jnp.bfloat16, jnp.float32


def y_place(y):
    return y % 2 * 2 + y // 2


def shift(value, axis, by):
    if axis == Y:
        pairs = [(y_place(i), y_place((i + by) % 4)) for i in range(4)]
    else:
        pairs = [(i, (i + by) % 4) for i in range(4)]
    return lax.ppermute(value, axis, pairs)


def swap(value, axis):
    return lax.ppermute(value, axis, [(0, 1), (1, 0)])


def from_three(value, axis):
    return [shift(value, axis, 1), shift(value, axis, -1), shift(value, axis, 2)]


def to_three(blocks, axis):
    return [shift(blocks[1], axis, -1), shift(blocks[2], axis, 1), shift(blocks[3], axis, 2)]


def total(first, *others):
    result = first.astype(F32)
    for other in others:
        result = result + other.astype(F32)
    return result


def attend(queries, keys, values, segment_ids):
    z = lax.axis_index("z")
    rows = queries.shape[0]
    seg_row = jnp.pad(segment_ids.astype(BF)[None, :], ((0, 7), (0, rows)))
    block = jnp.concatenate(
        [
            jnp.concatenate(
                [
                    lax.dynamic_slice_in_dim(keys, z * HD, HD, 1),
                    lax.dynamic_slice_in_dim(values, z * HD, HD, 1),
                ],
                axis=1,
            ),
            seg_row,
        ],
        axis=0,
    )
    x, yl, core = lax.axis_index("x"), lax.axis_index("yl"), lax.axis_index("core")
    blocks = jnp.stack([block] + from_three(block, X))
    blocks = jnp.stack([blocks, swap(blocks, "yl")])
    blocks = jnp.stack([blocks, swap(blocks, "core")])
    places = [
        ((x + dx) & 3) * 4 + ((yl + dy) & 1) * 2 + ((core + dc) & 1)
        for dc in (0, 1)
        for dy in (0, 1)
        for dx in (0, 3, 1, 2)
    ]
    blocks = blocks.reshape(16, rows + 8, 2 * HD)
    key_rows = blocks[:, :rows, :HD].reshape(16 * rows, HD)
    value_rows = blocks[:, :rows, HD:].reshape(16 * rows, HD)
    seg_keys = blocks[:, rows, :rows].reshape(16 * rows).astype(jnp.int32)
    row_ids = jnp.arange(rows, dtype=jnp.int32)
    key_pos = (jnp.stack(places)[:, None] * rows + row_ids[None, :]).reshape(16 * rows)
    query_pos = (x * 4 + yl * 2 + core) * rows + row_ids
    allowed = (key_pos[None, :] <= query_pos[:, None]) & (
        seg_keys[None, :] == segment_ids[:, None]
    )
    head_count = queries.shape[1] // HD
    query_heads = queries.reshape(rows, head_count, HD)
    scores = jnp.einsum("qrd,kd->rqk", query_heads, key_rows, preferred_element_type=F32)
    scores = jnp.where(allowed[None], scores * HD ** (-0.5), NEG_FILL)
    peak = jnp.max(scores, axis=-1, keepdims=True)
    weights = jnp.where(allowed[None], jnp.exp(scores - peak), 0.0)
    sums = jnp.sum(weights, axis=-1)
    update = jnp.einsum(
        "rqk,kd->rqd", weights.astype(BF), value_rows, preferred_element_type=F32
    )
    attention = (update / sums[..., None]).astype(BF)
    return attention.transpose(1, 0, 2).reshape(rows, head_count * HD)


def gather_plane(rows):
    half = rows.shape[1] // 2
    first, second = rows[:, :half], rows[:, half:]
    first = jnp.concatenate([first] + from_three(first, X))
    second = jnp.concatenate([second] + from_three(second, Y))
    return [first] + from_three(first, Y), [second] + from_three(second, X)


def scatter_plane(first, second):
    first_in = to_three([total(*terms).astype(BF) for terms in first], Y)
    second_in = to_three([total(*terms).astype(BF) for terms in second], X)
    first = total(*first[0], *first_in).astype(BF)
    second = total(*second[0], *second_in).astype(BF)
    first = first.reshape(4, -1, first.shape[-1])
    second = second.reshape(4, -1, second.shape[-1])
    first_in, second_in = to_three(first, X), to_three(second, Y)
    return jnp.concatenate(
        [total(first[0], *first_in).astype(BF), total(second[0], *second_in).astype(BF)], axis=1
    )


STEPS = 2


def turned(value):
    rows = value.shape[0] // 16
    return jnp.concatenate(
        [value[(j * 4 + i) * rows : (j * 4 + i + 1) * rows] for i in range(4) for j in range(4)]
    )


def expert_kernel(*refs):
    first_in, second_in = refs[0:4], refs[4:8]
    gate_ref, up_ref, down_ref = refs[8:11]
    first_out, second_out = refs[11:15], refs[15:19]
    sums, hidden = refs[19:]
    step = pl.program_id(0)
    units = gate_ref.shape[1]

    def add(which, blocks, fresh):
        rows = jnp.concatenate([block[...] for block in blocks])
        gate_val = jnp.dot(rows, gate_ref[...], preferred_element_type=F32)
        up_val = jnp.dot(rows, up_ref[...], preferred_element_type=F32)
        if fresh:
            sums[which, :, :units] = gate_val
            sums[which, :, units:] = up_val
        else:
            sums[which, :, :units] += gate_val
            sums[which, :, units:] += up_val

    def put(which, blocks):
        result = jnp.dot(hidden[which], down_ref[...], preferred_element_type=F32).astype(BF)
        rows = blocks[0].shape[0]
        for i, block in enumerate(blocks):
            block[...] = result[i * rows : (i + 1) * rows]

    for i in range(STEPS):
        pl.when(step == i)(lambda i=i: add(0, first_in, i == 0))
        pl.when(step == STEPS + i)(lambda i=i: add(1, second_in, i == 0))

    @pl.when(step == 2 * STEPS - 1)
    def _():
        both = sums[0] + turned(sums[1])
        gate_val, up_val = both[:, :units], both[:, units:]
        act = gate_val / (1.0 + jnp.exp(-gate_val)) * up_val
        hidden[0] = act.astype(BF)
        hidden[1] = turned(act).astype(BF)

    pl.when((step >= 2 * STEPS) & (step < 3 * STEPS))(lambda: put(0, first_out))
    pl.when(step >= 3 * STEPS)(lambda: put(1, second_out))


def expert(first, second, gate_weight, up_weight, down_weight):
    rows, half = first[0].shape
    features, units = gate_weight.shape
    wide = half // STEPS

    def column(at):
        return pl.BlockSpec((rows, wide), lambda i: (0, jnp.clip(i - at * STEPS, 0, STEPS - 1)))

    weight_in = pl.BlockSpec((wide, units), lambda i: (jnp.minimum(i, 2 * STEPS - 1), 0))
    weight_out = pl.BlockSpec((units, wide), lambda i: (0, jnp.maximum(i - 2 * STEPS, 0)))
    piece = jax.ShapeDtypeStruct((rows, half), BF)
    result = pl.pallas_call(
        expert_kernel,
        grid=(4 * STEPS,),
        in_specs=[column(0)] * 4 + [column(1)] * 4 + [weight_in, weight_in, weight_out],
        out_specs=[column(2)] * 4 + [column(3)] * 4,
        out_shape=[piece] * 8,
        scratch_shapes=[
            pltpu.VMEM((2, 4 * rows, 2 * units), F32),
            pltpu.VMEM((2, 4 * rows, units), BF),
        ],
        compiler_params=pltpu.CompilerParams(vmem_limit_bytes=40 * 1024 * 1024),
        cost_estimate=pl.CostEstimate(
            flops=6 * 4 * rows * features * units,
            bytes_accessed=2 * (3 * features * units + 8 * rows * features),
            transcendentals=4 * rows * units,
        ),
        name="expert",
    )(*first, *second, gate_weight, up_weight, down_weight)
    return result[:4], result[4:]


def shards(
    queries,
    keys,
    values,
    segment_ids,
    residual,
    w_out,
    norm_gain,
    w_router,
    routes,
    w_gate,
    w_up,
    w_down,
):
    w_out_all = lax.all_gather(w_out, CTX, axis=1, tiled=True)
    attention = attend(queries, keys, values, segment_ids)
    head_partial = jnp.dot(attention, w_out_all, preferred_element_type=F32).astype(BF)
    width = head_partial.shape[1]
    tokens = routes.shape[0]

    route_flat = routes.reshape(-1)
    expert_ids = jnp.arange(EXPERTS, dtype=jnp.int32)
    onehot = (route_flat[:, None] == expert_ids).astype(jnp.int32)
    ranks = jnp.sum((jnp.cumsum(onehot, axis=0) - onehot) * onehot, axis=-1)
    slot_of_route = (route_flat * SLOTS + ranks).reshape(tokens, 2)
    slot_ids = jnp.arange(EXPERTS * SLOTS, dtype=jnp.int32)
    hot = slot_of_route[:, :, None] == slot_ids
    picks = jnp.any(hot, axis=1).astype(BF)
    head_partial, picks, hot = lax.optimization_barrier((head_partial, picks, hot))

    head_terms = lax.all_to_all(
        head_partial.reshape(16, tokens, width), EXP, split_axis=0, concat_axis=0, tiled=True
    )
    mixed = residual.astype(F32) + jnp.sum(head_terms.astype(F32), axis=0)
    normed = (
        mixed * lax.rsqrt(jnp.mean(mixed * mixed, axis=-1, keepdims=True) + EPSILON) * norm_gain
    ).astype(BF)

    outgoing = jnp.dot(picks.T, normed, preferred_element_type=F32).astype(BF)

    incoming = lax.all_to_all(
        outgoing.reshape(EXPERTS, SLOTS, width), "z", split_axis=0, concat_axis=0, tiled=True
    ).reshape(EXPERTS * SLOTS, width)
    first, second = gather_plane(incoming)
    other_first = [swap(block, "core") for block in first]
    other_second = [swap(block, "core") for block in second]
    weights = w_gate[0], w_up[0], w_down[0]
    first, second = expert(first, second, *weights)
    other_first, other_second = expert(other_first, other_second, *weights)
    slot_sums = scatter_plane(
        [(mine, swap(block, "core")) for mine, block in zip(first, other_first)],
        [(mine, swap(block, "core")) for mine, block in zip(second, other_second)],
    )
    logits = jnp.dot(normed, w_router, preferred_element_type=F32)
    chosen = jnp.sum((routes[..., None] == expert_ids).astype(F32) * logits[:, None, :], axis=-1)
    gates = jax.nn.softmax(chosen, axis=-1)
    slot_gates = jnp.sum(jnp.where(hot, gates[:, :, None], 0.0), axis=1)
    slot_sums, slot_gates = lax.optimization_barrier((slot_sums, slot_gates))
    returned = lax.all_to_all(
        slot_sums.reshape(EXPERTS, SLOTS, width), "z", split_axis=0, concat_axis=0, tiled=True
    ).reshape(EXPERTS * SLOTS, width)

    mixture = jnp.dot(
        slot_gates,
        returned.astype(F32),
        precision=lax.Precision.HIGHEST,
        preferred_element_type=F32,
    )
    return (mixed + mixture).astype(BF)


def solution(mesh):
    fine = Mesh(mesh.devices.reshape(4, 2, 2, 8, 2), ("x", "yl", "core", "z", "yh"))
    both = CTX + EXP
    placed = (
        P(CTX, EXP),
        P(CTX, None),
        P(CTX, None),
        P(CTX),
        P(both, None),
        P(EXP, CTX),
        P(),
        P(),
        P(both, None),
        P(EXP, None, CTX),
        P(EXP, None, CTX),
        P(EXP, CTX, None),
    )
    return jax.shard_map(
        shards, mesh=fine, in_specs=placed, out_specs=P(both, None), check_vma=False
    )
```

```python
import jax
import jax.numpy as jnp
import numpy as np
from jax import lax
from jax.experimental import pallas as pl
from jax.experimental.pallas import tpu as pltpu
from jax.sharding import Mesh, PartitionSpec as P

HEADS = 48
KVH = 8
HD = 128
EXPERTS = 8
NEG_FILL = -1e30
EPSILON = 1e-05
SLOTS = 3

X, CTX, EXP, Y = "x", ("x", "yl", "core"), ("z", "yh"), ("yl", "yh")
BF, F32 = jnp.bfloat16, jnp.float32


def y_place(y):
    return y % 2 * 2 + y // 2


def shift(value, axis, by):
    if axis == Y:
        pairs = [(y_place(i), y_place((i + by) % 4)) for i in range(4)]
    else:
        pairs = [(i, (i + by) % 4) for i in range(4)]
    return lax.ppermute(value, axis, pairs)


def swap(value, axis):
    return lax.ppermute(value, axis, [(0, 1), (1, 0)])


def after(value, *earlier):
    return lax.optimization_barrier((value,) + earlier)[0]


def from_three(value, axis):
    return [shift(value, axis, 1), shift(value, axis, -1), shift(value, axis, 2)]


def from_both(first, second, first_axis, second_axis):
    first_in = [shift(first, first_axis, 1), shift(first, first_axis, -1)]
    second_in = [shift(second, second_axis, 1), shift(second, second_axis, -1)]
    first_in.append(shift(after(first, first_in[0], second_in[0]), first_axis, 2))
    second_in.append(shift(after(second, first_in[1], second_in[1]), second_axis, 2))
    return first_in, second_in


def to_both(first, second, first_axis, second_axis):
    first_in = [shift(first[1], first_axis, -1), shift(first[2], first_axis, 1)]
    second_in = [shift(second[1], second_axis, -1), shift(second[2], second_axis, 1)]
    first_in.append(shift(after(first[3], first_in[0], second_in[0]), first_axis, 2))
    second_in.append(shift(after(second[3], first_in[1], second_in[1]), second_axis, 2))
    return first_in, second_in


def total(first, *others):
    result = first.astype(F32)
    for other in others:
        result = result + other.astype(F32)
    return result


def attend(queries, keys, values, segment_ids):
    z = lax.axis_index("z")
    rows = queries.shape[0]
    seg_row = jnp.pad(segment_ids.astype(BF)[None, :], ((0, 7), (0, rows)))
    block = jnp.concatenate(
        [
            jnp.concatenate(
                [
                    lax.dynamic_slice_in_dim(keys, z * HD, HD, 1),
                    lax.dynamic_slice_in_dim(values, z * HD, HD, 1),
                ],
                axis=1,
            ),
            seg_row,
        ],
        axis=0,
    )
    x, yl, core = lax.axis_index("x"), lax.axis_index("yl"), lax.axis_index("core")
    blocks = jnp.stack([block] + from_three(block, X))
    blocks = jnp.stack([blocks, swap(blocks, "yl")])
    blocks = jnp.stack([blocks, swap(blocks, "core")])
    places = [
        ((x + dx) & 3) * 4 + ((yl + dy) & 1) * 2 + ((core + dc) & 1)
        for dc in (0, 1)
        for dy in (0, 1)
        for dx in (0, 3, 1, 2)
    ]
    blocks = blocks.reshape(16, rows + 8, 2 * HD)
    key_rows = blocks[:, :rows, :HD].reshape(16 * rows, HD)
    value_rows = blocks[:, :rows, HD:].reshape(16 * rows, HD)
    seg_keys = blocks[:, rows, :rows].reshape(16 * rows).astype(jnp.int32)
    row_ids = jnp.arange(rows, dtype=jnp.int32)
    key_pos = (jnp.stack(places)[:, None] * rows + row_ids[None, :]).reshape(16 * rows)
    query_pos = (x * 4 + yl * 2 + core) * rows + row_ids
    allowed = (key_pos[None, :] <= query_pos[:, None]) & (
        seg_keys[None, :] == segment_ids[:, None]
    )
    head_count = queries.shape[1] // HD
    query_heads = queries.reshape(rows, head_count, HD)
    scores = jnp.einsum("qrd,kd->rqk", query_heads, key_rows, preferred_element_type=F32)
    scores = jnp.where(allowed[None], scores * HD ** (-0.5), NEG_FILL)
    peak = jnp.max(scores, axis=-1, keepdims=True)
    weights = jnp.where(allowed[None], jnp.exp(scores - peak), 0.0)
    sums = jnp.sum(weights, axis=-1)
    update = jnp.einsum(
        "rqk,kd->rqd", weights.astype(BF), value_rows, preferred_element_type=F32
    )
    attention = (update / sums[..., None]).astype(BF)
    return attention.transpose(1, 0, 2).reshape(rows, head_count * HD)


def gather_plane(rows):
    half = rows.shape[1] // 2
    first, second = rows[:, :half], rows[:, half:]
    first_in, second_in = from_both(first, second, X, Y)
    first_in, second_in = lax.optimization_barrier((first_in, second_in))
    first, second = jnp.concatenate([first] + first_in), jnp.concatenate([second] + second_in)
    first_in, second_in = from_both(first, second, Y, X)
    first_other = [swap(after(first, first_in[0]), "core")]
    second_other = [swap(after(second, second_in[0]), "core")]
    first_other += [swap(block, "core") for block in first_in]
    second_other += [swap(block, "core") for block in second_in]
    return [first] + first_in, [second] + second_in, first_other, second_other


def own_swap(blocks, arrived):
    return swap(after(blocks[0][1], arrived[0]), "core")


def scatter_plane(first, second):
    sent = [[total(*terms).astype(BF) for terms in blocks[1:3]] for blocks in (first, second)]
    (first_one, first_two), (second_one, second_two) = lax.optimization_barrier(sent)
    first_in, second_in = to_both(
        [None, first_one, first_two, total(*first[3]).astype(BF)],
        [None, second_one, second_two, total(*second[3]).astype(BF)],
        Y,
        X,
    )
    first = total(first[0][0], own_swap(first, first_in), *first_in).astype(BF)
    second = total(second[0][0], own_swap(second, second_in), *second_in).astype(BF)
    first, second = lax.optimization_barrier((first, second))
    first = first.reshape(4, -1, first.shape[-1])
    second = second.reshape(4, -1, second.shape[-1])
    first_in, second_in = to_both(first, second, X, Y)
    return jnp.concatenate(
        [total(first[0], *first_in).astype(BF), total(second[0], *second_in).astype(BF)], axis=1
    )


STEPS = 1


def turned(value):
    rows = value.shape[0] // 16
    return jnp.concatenate(
        [value[(j * 4 + i) * rows : (j * 4 + i + 1) * rows] for i in range(4) for j in range(4)]
    )


def expert_kernel(*refs):
    first_in, second_in = refs[0:4], refs[4:8]
    gate_ref, up_ref, down_ref = refs[8:11]
    first_out, second_out = refs[11:15], refs[15:19]
    sums, hidden = refs[19:]
    step = pl.program_id(0)
    units = gate_ref.shape[1]

    def add(which, blocks, fresh):
        rows = jnp.concatenate([block[...] for block in blocks])
        gate_val = jnp.dot(rows, gate_ref[...], preferred_element_type=F32)
        up_val = jnp.dot(rows, up_ref[...], preferred_element_type=F32)
        if fresh:
            sums[which, :, :units] = gate_val
            sums[which, :, units:] = up_val
        else:
            sums[which, :, :units] += gate_val
            sums[which, :, units:] += up_val

    def put(which, blocks):
        result = jnp.dot(hidden[which], down_ref[...], preferred_element_type=F32).astype(BF)
        rows = blocks[0].shape[0]
        for i, block in enumerate(blocks):
            block[...] = result[i * rows : (i + 1) * rows]

    for i in range(STEPS):
        pl.when(step == i)(lambda i=i: add(0, first_in, i == 0))
        pl.when(step == STEPS + i)(lambda i=i: add(1, second_in, i == 0))

    @pl.when(step == 2 * STEPS - 1)
    def _():
        both = sums[0] + turned(sums[1])
        gate_val, up_val = both[:, :units], both[:, units:]
        act = gate_val / (1.0 + jnp.exp(-gate_val)) * up_val
        hidden[0] = act.astype(BF)
        hidden[1] = turned(act).astype(BF)

    pl.when((step >= 2 * STEPS) & (step < 3 * STEPS))(lambda: put(0, first_out))
    pl.when(step >= 3 * STEPS)(lambda: put(1, second_out))


def expert(first, second, gate_weight, up_weight, down_weight):
    rows, half = first[0].shape
    features, units = gate_weight.shape
    wide = half // STEPS

    def column(at):
        return pl.BlockSpec((rows, wide), lambda i: (0, jnp.clip(i - at * STEPS, 0, STEPS - 1)))

    weight_in = pl.BlockSpec((wide, units), lambda i: (jnp.minimum(i, 2 * STEPS - 1), 0))
    weight_out = pl.BlockSpec((units, wide), lambda i: (0, jnp.maximum(i - 2 * STEPS, 0)))
    piece = jax.ShapeDtypeStruct((rows, half), BF)
    result = pl.pallas_call(
        expert_kernel,
        grid=(4 * STEPS,),
        in_specs=[column(0)] * 4 + [column(1)] * 4 + [weight_in, weight_in, weight_out],
        out_specs=[column(2)] * 4 + [column(3)] * 4,
        out_shape=[piece] * 8,
        scratch_shapes=[
            pltpu.VMEM((2, 4 * rows, 2 * units), F32),
            pltpu.VMEM((2, 4 * rows, units), BF),
        ],
        compiler_params=pltpu.CompilerParams(vmem_limit_bytes=40 * 1024 * 1024),
        cost_estimate=pl.CostEstimate(
            flops=6 * 4 * rows * features * units,
            bytes_accessed=2 * (3 * features * units + 8 * rows * features),
            transcendentals=4 * rows * units,
        ),
        name="expert",
    )(*first, *second, gate_weight, up_weight, down_weight)
    return result[:4], result[4:]


def shards(
    queries,
    keys,
    values,
    segment_ids,
    residual,
    w_out,
    norm_gain,
    w_router,
    routes,
    w_gate,
    w_up,
    w_down,
):
    w_out_all = lax.all_gather(w_out, CTX, axis=1, tiled=True)
    attention = attend(queries, keys, values, segment_ids)
    head_partial = jnp.dot(attention, w_out_all, preferred_element_type=F32).astype(BF)
    width = head_partial.shape[1]
    tokens = routes.shape[0]

    route_flat = routes.reshape(-1)
    expert_ids = jnp.arange(EXPERTS, dtype=jnp.int32)
    onehot = (route_flat[:, None] == expert_ids).astype(jnp.int32)
    ranks = jnp.sum((jnp.cumsum(onehot, axis=0) - onehot) * onehot, axis=-1)
    slot_of_route = (route_flat * SLOTS + ranks).reshape(tokens, 2)
    slot_ids = jnp.arange(EXPERTS * SLOTS, dtype=jnp.int32)
    hot = slot_of_route[:, :, None] == slot_ids
    picks = jnp.any(hot, axis=1).astype(BF)
    head_partial, picks, hot = lax.optimization_barrier((head_partial, picks, hot))

    head_terms = lax.all_to_all(
        head_partial.reshape(16, tokens, width), EXP, split_axis=0, concat_axis=0, tiled=True
    )
    mixed = residual.astype(F32) + jnp.sum(head_terms.astype(F32), axis=0)
    normed = (
        mixed * lax.rsqrt(jnp.mean(mixed * mixed, axis=-1, keepdims=True) + EPSILON) * norm_gain
    ).astype(BF)

    outgoing = jnp.dot(picks.T, normed, preferred_element_type=F32).astype(BF)

    incoming = lax.all_to_all(
        outgoing.reshape(EXPERTS, SLOTS, width), "z", split_axis=0, concat_axis=0, tiled=True
    ).reshape(EXPERTS * SLOTS, width)
    first, second, other_first, other_second = gather_plane(incoming)
    weights = w_gate[0], w_up[0], w_down[0]
    first, second = expert(first, second, *weights)
    other_first, other_second = expert(other_first, other_second, *weights)
    slot_sums = scatter_plane(
        [(first[0], other_first[0])]
        + [(mine, swap(block, "core")) for mine, block in zip(first[1:], other_first[1:])],
        [(second[0], other_second[0])]
        + [(mine, swap(block, "core")) for mine, block in zip(second[1:], other_second[1:])],
    )
    logits = jnp.dot(normed, w_router, preferred_element_type=F32)
    chosen = jnp.sum((routes[..., None] == expert_ids).astype(F32) * logits[:, None, :], axis=-1)
    gates = jax.nn.softmax(chosen, axis=-1)
    slot_gates = jnp.sum(jnp.where(hot, gates[:, :, None], 0.0), axis=1)
    slot_sums, slot_gates = lax.optimization_barrier((slot_sums, slot_gates))
    returned = lax.all_to_all(
        slot_sums.reshape(EXPERTS, SLOTS, width), "z", split_axis=0, concat_axis=0, tiled=True
    ).reshape(EXPERTS * SLOTS, width)

    mixture = jnp.dot(
        slot_gates,
        returned.astype(F32),
        precision=lax.Precision.HIGHEST,
        preferred_element_type=F32,
    )
    return (mixed + mixture).astype(BF)


def solution(mesh):
    fine = Mesh(mesh.devices.reshape(4, 2, 2, 8, 2), ("x", "yl", "core", "z", "yh"))
    both = CTX + EXP
    placed = (
        P(CTX, EXP),
        P(CTX, None),
        P(CTX, None),
        P(CTX),
        P(both, None),
        P(EXP, CTX),
        P(),
        P(),
        P(both, None),
        P(EXP, None, CTX),
        P(EXP, None, CTX),
        P(EXP, CTX, None),
    )
    return jax.shard_map(
        shards, mesh=fine, in_specs=placed, out_specs=P(both, None), check_vma=False
    )
```

```python
import functools

import jax
import jax.numpy as jnp
import numpy as np
from jax import lax
from jax.experimental import pallas as pl
from jax.experimental.pallas import tpu as pltpu
from jax.sharding import Mesh, PartitionSpec as P

HEADS = 48
KVH = 8
HD = 128
EXPERTS = 8
NEG_FILL = -1e30
EPSILON = 1e-05
SLOTS = 3

CTX, EXP, PLANE = ("x", "yl", "core"), ("z", "yh"), ("x", "yl", "core", "yh")
BF, F32 = jnp.bfloat16, jnp.float32


def swap(value, axis):
    return lax.ppermute(value, axis, [(0, 1), (1, 0)])


def plane_shift(value, by, turn):
    def index(x, y, core):
        return ((x * 2 + y % 2) * 2 + core) * 2 + y // 2

    pairs = [
        (
            index(x, y, core),
            index((x + by) % 4, y, core) if core == turn else index(x, (y + by) % 4, core),
        )
        for x in range(4)
        for y in range(4)
        for core in (0, 1)
    ]
    return lax.ppermute(value, PLANE, pairs)


def total(first, *others):
    result = first.astype(F32)
    for other in others:
        result = result + other.astype(F32)
    return result


def attend(queries, keys, values, segment_ids):
    z = lax.axis_index("z")
    rows = queries.shape[0]
    seg_row = jnp.pad(segment_ids.astype(BF)[None, :], ((0, 7), (0, rows)))
    block = jnp.concatenate(
        [
            jnp.concatenate(
                [
                    lax.dynamic_slice_in_dim(keys, z * HD, HD, 1),
                    lax.dynamic_slice_in_dim(values, z * HD, HD, 1),
                ],
                axis=1,
            ),
            seg_row,
        ],
        axis=0,
    )
    x, yl, core = lax.axis_index("x"), lax.axis_index("yl"), lax.axis_index("core")
    along_x = [lax.ppermute(block, "x", [(i, (i + by) % 4) for i in range(4)]) for by in (1, 3, 2)]
    blocks = jnp.stack([block] + along_x)
    blocks = jnp.stack([blocks, swap(blocks, "yl")])
    blocks = jnp.stack([blocks, swap(blocks, "core")])
    places = [
        ((x + dx) & 3) * 4 + ((yl + dy) & 1) * 2 + ((core + dc) & 1)
        for dc in (0, 1)
        for dy in (0, 1)
        for dx in (0, 3, 1, 2)
    ]
    blocks = blocks.reshape(16, rows + 8, 2 * HD)
    key_rows = blocks[:, :rows, :HD].reshape(16 * rows, HD)
    value_rows = blocks[:, :rows, HD:].reshape(16 * rows, HD)
    seg_keys = blocks[:, rows, :rows].reshape(16 * rows).astype(jnp.int32)
    row_ids = jnp.arange(rows, dtype=jnp.int32)
    key_pos = (jnp.stack(places)[:, None] * rows + row_ids[None, :]).reshape(16 * rows)
    query_pos = (x * 4 + yl * 2 + core) * rows + row_ids
    allowed = (key_pos[None, :] <= query_pos[:, None]) & (
        seg_keys[None, :] == segment_ids[:, None]
    )
    head_count = queries.shape[1] // HD
    query_heads = queries.reshape(rows, head_count, HD)
    scores = jnp.einsum("qrd,kd->rqk", query_heads, key_rows, preferred_element_type=F32)
    scores = jnp.where(allowed[None], scores * HD ** (-0.5), NEG_FILL)
    peak = jnp.max(scores, axis=-1, keepdims=True)
    weights = jnp.where(allowed[None], jnp.exp(scores - peak), 0.0)
    sums = jnp.sum(weights, axis=-1)
    update = jnp.einsum(
        "rqk,kd->rqd", weights.astype(BF), value_rows, preferred_element_type=F32
    )
    attention = (update / sums[..., None]).astype(BF)
    return attention.transpose(1, 0, 2).reshape(rows, head_count * HD)


def gather_plane(rows):
    near = [plane_shift(rows, by, 0) for by in (1, -1, 2)]
    rows = jnp.concatenate([rows] + near)
    half = rows.shape[0] // 2
    left, right = plane_shift(rows, 1, 1), plane_shift(rows, -1, 1)
    far_first = plane_shift(left[:half], 1, 1)
    far_second = plane_shift(right[half:], -1, 1)
    mine = [rows, left, right, far_first, far_second]
    return mine, [swap(block, "core") for block in mine]


def scatter_plane(mine, other):
    far_first, far_second = [total(mine[i], swap(other[i], "core")).astype(BF) for i in (3, 4)]
    far_first, far_second = lax.optimization_barrier((far_first, far_second))
    half = far_first.shape[0]
    far_first, far_second = plane_shift(far_first, -1, 1), plane_shift(far_second, 1, 1)
    left, right = [total(mine[i], swap(other[i], "core")) for i in (1, 2)]
    left = jnp.concatenate([left[:half] + far_first.astype(F32), left[half:]]).astype(BF)
    right = jnp.concatenate([right[:half], right[half:] + far_second.astype(F32)]).astype(BF)
    left, right = lax.optimization_barrier((left, right))
    left, right = plane_shift(left, -1, 1), plane_shift(right, 1, 1)
    rows = total(mine[0], swap(other[0], "core"), left, right).astype(BF)
    rows = rows.reshape(4, -1, rows.shape[-1])
    near = [plane_shift(rows[i], by, 0) for i, by in ((1, -1), (2, 1), (3, 2))]
    return total(rows[0], *near).astype(BF)


STEPS = 2


def expert_kernel(count, *refs):
    rows_in, (gate_ref, up_ref, down_ref) = refs[:count], refs[count : count + 3]
    rows_out, (sums, hidden) = refs[count + 3 : 2 * count + 3], refs[2 * count + 3 :]
    step = pl.program_id(0)
    units = gate_ref.shape[1]

    def add(fresh):
        rows = jnp.concatenate([block[...] for block in rows_in])
        gate_val = jnp.dot(rows, gate_ref[...], preferred_element_type=F32)
        up_val = jnp.dot(rows, up_ref[...], preferred_element_type=F32)
        if fresh:
            sums[:, :units] = gate_val
            sums[:, units:] = up_val
        else:
            sums[:, :units] += gate_val
            sums[:, units:] += up_val

    pl.when(step == 0)(lambda: add(True))
    pl.when((step > 0) & (step < STEPS))(lambda: add(False))

    @pl.when(step == STEPS - 1)
    def _():
        gate_val, up_val = sums[:, :units], sums[:, units:]
        hidden[...] = (gate_val / (1.0 + jnp.exp(-gate_val)) * up_val).astype(BF)

    @pl.when(step >= STEPS)
    def _():
        result = jnp.dot(hidden[...], down_ref[...], preferred_element_type=F32).astype(BF)
        first = 0
        for block in rows_out:
            block[...] = result[first : first + block.shape[0]]
            first += block.shape[0]


def expert(blocks, gate_weight, up_weight, down_weight):
    features, units = gate_weight.shape
    rows = sum(block.shape[0] for block in blocks)
    wide = features // STEPS
    lead, trail = lambda i: jnp.minimum(i, STEPS - 1), lambda i: jnp.maximum(i - STEPS, 0)
    weight_in = pl.BlockSpec((wide, units), lambda i: (lead(i), 0))
    weight_out = pl.BlockSpec((units, wide), lambda i: (0, trail(i)))
    return pl.pallas_call(
        functools.partial(expert_kernel, len(blocks)),
        grid=(2 * STEPS,),
        in_specs=[pl.BlockSpec((b.shape[0], wide), lambda i: (0, lead(i))) for b in blocks]
        + [weight_in, weight_in, weight_out],
        out_specs=[pl.BlockSpec((b.shape[0], wide), lambda i: (0, trail(i))) for b in blocks],
        out_shape=[jax.ShapeDtypeStruct(b.shape, BF) for b in blocks],
        scratch_shapes=[pltpu.VMEM((rows, 2 * units), F32), pltpu.VMEM((rows, units), BF)],
        compiler_params=pltpu.CompilerParams(vmem_limit_bytes=40 * 1024 * 1024),
        cost_estimate=pl.CostEstimate(
            flops=6 * rows * features * units,
            bytes_accessed=2 * (3 * features * units + 2 * rows * features),
            transcendentals=rows * units,
        ),
        name="expert",
    )(*blocks, gate_weight, up_weight, down_weight)


def shards(
    queries,
    keys,
    values,
    segment_ids,
    residual,
    w_out,
    norm_gain,
    w_router,
    routes,
    w_gate,
    w_up,
    w_down,
):
    w_out_all = lax.all_gather(w_out, CTX, axis=1, tiled=True)
    attention = attend(queries, keys, values, segment_ids)
    head_partial = jnp.dot(attention, w_out_all, preferred_element_type=F32).astype(BF)
    width = head_partial.shape[1]
    tokens = routes.shape[0]

    route_flat = routes.reshape(-1)
    expert_ids = jnp.arange(EXPERTS, dtype=jnp.int32)
    onehot = (route_flat[:, None] == expert_ids).astype(jnp.int32)
    ranks = jnp.sum((jnp.cumsum(onehot, axis=0) - onehot) * onehot, axis=-1)
    slot_of_route = (route_flat * SLOTS + ranks).reshape(tokens, 2)
    slot_ids = jnp.arange(EXPERTS * SLOTS, dtype=jnp.int32)
    hot = slot_of_route[:, :, None] == slot_ids
    picks = jnp.any(hot, axis=1).astype(BF)
    head_partial, picks, hot = lax.optimization_barrier((head_partial, picks, hot))

    head_terms = lax.all_to_all(
        head_partial.reshape(16, tokens, width), EXP, split_axis=0, concat_axis=0, tiled=True
    )
    mixed = residual.astype(F32) + jnp.sum(head_terms.astype(F32), axis=0)
    normed = (
        mixed * lax.rsqrt(jnp.mean(mixed * mixed, axis=-1, keepdims=True) + EPSILON) * norm_gain
    ).astype(BF)

    outgoing = jnp.dot(picks.T, normed, preferred_element_type=F32).astype(BF)

    incoming = lax.all_to_all(
        outgoing.reshape(EXPERTS, SLOTS, width), "z", split_axis=0, concat_axis=0, tiled=True
    ).reshape(EXPERTS * SLOTS, width)
    mine, other = gather_plane(incoming)
    weights = w_gate[0], w_up[0], w_down[0]
    slot_sums = scatter_plane(expert(mine, *weights), expert(other, *weights))
    logits = jnp.dot(normed, w_router, preferred_element_type=F32)
    chosen = jnp.sum((routes[..., None] == expert_ids).astype(F32) * logits[:, None, :], axis=-1)
    gates = jax.nn.softmax(chosen, axis=-1)
    slot_gates = jnp.sum(jnp.where(hot, gates[:, :, None], 0.0), axis=1)
    slot_sums, slot_gates = lax.optimization_barrier((slot_sums, slot_gates))
    returned = lax.all_to_all(
        slot_sums.reshape(EXPERTS, SLOTS, width), "z", split_axis=0, concat_axis=0, tiled=True
    ).reshape(EXPERTS * SLOTS, width)

    mixture = jnp.dot(
        slot_gates,
        returned.astype(F32),
        precision=lax.Precision.HIGHEST,
        preferred_element_type=F32,
    )
    return (mixed + mixture).astype(BF)


def solution(mesh):
    fine = Mesh(mesh.devices.reshape(4, 2, 2, 8, 2), ("x", "yl", "core", "z", "yh"))
    both = CTX + EXP
    placed = (
        P(CTX, EXP),
        P(CTX, None),
        P(CTX, None),
        P(CTX),
        P(both, None),
        P(EXP, CTX),
        P(),
        P(),
        P(both, None),
        P(EXP, None, CTX),
        P(EXP, None, CTX),
        P(EXP, CTX, None),
    )
    return jax.shard_map(
        shards, mesh=fine, in_specs=placed, out_specs=P(both, None), check_vma=False
    )
```

```python
import functools

import jax
import jax.numpy as jnp
import numpy as np
from jax import lax
from jax.experimental import pallas as pl
from jax.experimental.pallas import tpu as pltpu
from jax.sharding import Mesh, PartitionSpec as P

HEADS = 48
KVH = 8
HD = 128
EXPERTS = 8
NEG_FILL = -1e30
EPSILON = 1e-05
SLOTS = 3

CTX, EXP, PLANE = ("x", "yl", "core"), ("z", "yh"), ("x", "yl", "core", "yh")
BF, F32 = jnp.bfloat16, jnp.float32


def swap(value, axis):
    return lax.ppermute(value, axis, [(0, 1), (1, 0)])


def plane_shift(value, by, turn):
    def index(x, y, core):
        return ((x * 2 + y % 2) * 2 + core) * 2 + y // 2

    pairs = [
        (
            index(x, y, core),
            index((x + by) % 4, y, core) if core == turn else index(x, (y + by) % 4, core),
        )
        for x in range(4)
        for y in range(4)
        for core in (0, 1)
    ]
    return lax.ppermute(value, PLANE, pairs)


def after(values, *earlier):
    return lax.optimization_barrier((values, earlier))[0]


def total(first, *others):
    result = first.astype(F32)
    for other in others:
        result = result + other.astype(F32)
    return result


def attend(queries, keys, values, segment_ids):
    z = lax.axis_index("z")
    rows = queries.shape[0]
    seg_row = jnp.pad(segment_ids.astype(BF)[None, :], ((0, 7), (0, rows)))
    block = jnp.concatenate(
        [
            jnp.concatenate(
                [
                    lax.dynamic_slice_in_dim(keys, z * HD, HD, 1),
                    lax.dynamic_slice_in_dim(values, z * HD, HD, 1),
                ],
                axis=1,
            ),
            seg_row,
        ],
        axis=0,
    )
    x, yl, core = lax.axis_index("x"), lax.axis_index("yl"), lax.axis_index("core")
    along_x = [lax.ppermute(block, "x", [(i, (i + by) % 4) for i in range(4)]) for by in (1, 3, 2)]
    blocks = jnp.stack([block] + along_x)
    blocks = jnp.stack([blocks, swap(blocks, "yl")])
    blocks = jnp.stack([blocks, swap(blocks, "core")])
    places = [
        ((x + dx) & 3) * 4 + ((yl + dy) & 1) * 2 + ((core + dc) & 1)
        for dc in (0, 1)
        for dy in (0, 1)
        for dx in (0, 3, 1, 2)
    ]
    blocks = blocks.reshape(16, rows + 8, 2 * HD)
    key_rows = blocks[:, :rows, :HD].reshape(16 * rows, HD)
    value_rows = blocks[:, :rows, HD:].reshape(16 * rows, HD)
    seg_keys = blocks[:, rows, :rows].reshape(16 * rows).astype(jnp.int32)
    row_ids = jnp.arange(rows, dtype=jnp.int32)
    key_pos = (jnp.stack(places)[:, None] * rows + row_ids[None, :]).reshape(16 * rows)
    query_pos = (x * 4 + yl * 2 + core) * rows + row_ids
    allowed = (key_pos[None, :] <= query_pos[:, None]) & (
        seg_keys[None, :] == segment_ids[:, None]
    )
    head_count = queries.shape[1] // HD
    query_heads = queries.reshape(rows, head_count, HD)
    scores = jnp.einsum("qrd,kd->rqk", query_heads, key_rows, preferred_element_type=F32)
    scores = jnp.where(allowed[None], scores * HD ** (-0.5), NEG_FILL)
    peak = jnp.max(scores, axis=-1, keepdims=True)
    weights = jnp.where(allowed[None], jnp.exp(scores - peak), 0.0)
    sums = jnp.sum(weights, axis=-1)
    update = jnp.einsum(
        "rqk,kd->rqd", weights.astype(BF), value_rows, preferred_element_type=F32
    )
    attention = (update / sums[..., None]).astype(BF)
    return attention.transpose(1, 0, 2).reshape(rows, head_count * HD)


def plane_experts(rows, expert_of):
    near = [plane_shift(rows, by, 0) for by in (1, -1, 2)]
    rows = jnp.concatenate([rows] + near)
    half = rows.shape[0] // 2
    first, second = rows[:half], rows[half:]
    left_first, right_second = plane_shift(first, 1, 1), plane_shift(second, -1, 1)
    left_second, right_first = plane_shift(second, 1, 1), plane_shift(first, -1, 1)
    far_first, far_second = plane_shift(left_first, 1, 1), plane_shift(right_second, -1, 1)
    mine = [rows, left_first, left_second, right_first, right_second]
    far = [far_first, far_second]
    other = [swap(block, "core") for block in after(mine, right_first)]
    other_far = [swap(block, "core") for block in far]

    mine, other = expert_of(mine), expert_of(other)
    left_second = total(mine[2], swap(other[2], "core")).astype(BF)
    right_first = total(mine[3], swap(other[3], "core")).astype(BF)
    far = expert_of(far + other_far)
    left_first, right_second = [total(mine[i], swap(other[i], "core")) for i in (1, 4)]
    far_first, far_second = [total(far[i], swap(far[i + 2], "core")).astype(BF) for i in (0, 1)]
    far_first, far_second = plane_shift(far_first, -1, 1), plane_shift(far_second, 1, 1)
    left_second, right_first = plane_shift(left_second, -1, 1), plane_shift(right_first, 1, 1)
    left_first = plane_shift((left_first + far_first.astype(F32)).astype(BF), -1, 1)
    right_second = plane_shift((right_second + far_second.astype(F32)).astype(BF), 1, 1)
    own = total(mine[0], swap(after(other[0], far_first), "core"))
    first = own[:half] + total(left_first, right_first)
    second = own[half:] + total(left_second, right_second)
    first, second = [value.astype(BF).reshape(2, half // 2, -1) for value in (first, second)]
    near = [plane_shift(block, by, 0) for block, by in ((first[1], -1), (second[0], 1), (second[1], 2))]
    return total(first[0], *near).astype(BF)


STEPS = 2


def expert_kernel(count, *refs):
    rows_in, (gate_ref, up_ref, down_ref) = refs[:count], refs[count : count + 3]
    rows_out, (sums, hidden) = refs[count + 3 : 2 * count + 3], refs[2 * count + 3 :]
    step = pl.program_id(0)
    units = gate_ref.shape[1]

    def add(fresh):
        rows = jnp.concatenate([block[...] for block in rows_in])
        gate_val = jnp.dot(rows, gate_ref[...], preferred_element_type=F32)
        up_val = jnp.dot(rows, up_ref[...], preferred_element_type=F32)
        if fresh:
            sums[:, :units] = gate_val
            sums[:, units:] = up_val
        else:
            sums[:, :units] += gate_val
            sums[:, units:] += up_val

    pl.when(step == 0)(lambda: add(True))
    pl.when((step > 0) & (step < STEPS))(lambda: add(False))

    @pl.when(step == STEPS - 1)
    def _():
        gate_val, up_val = sums[:, :units], sums[:, units:]
        hidden[...] = (gate_val / (1.0 + jnp.exp(-gate_val)) * up_val).astype(BF)

    @pl.when(step >= STEPS)
    def _():
        result = jnp.dot(hidden[...], down_ref[...], preferred_element_type=F32).astype(BF)
        first = 0
        for block in rows_out:
            block[...] = result[first : first + block.shape[0]]
            first += block.shape[0]


def expert(blocks, gate_weight, up_weight, down_weight):
    features, units = gate_weight.shape
    rows = sum(block.shape[0] for block in blocks)
    wide = features // STEPS
    lead, trail = lambda i: jnp.minimum(i, STEPS - 1), lambda i: jnp.maximum(i - STEPS, 0)
    weight_in = pl.BlockSpec((wide, units), lambda i: (lead(i), 0))
    weight_out = pl.BlockSpec((units, wide), lambda i: (0, trail(i)))
    return pl.pallas_call(
        functools.partial(expert_kernel, len(blocks)),
        grid=(2 * STEPS,),
        in_specs=[pl.BlockSpec((b.shape[0], wide), lambda i: (0, lead(i))) for b in blocks]
        + [weight_in, weight_in, weight_out],
        out_specs=[pl.BlockSpec((b.shape[0], wide), lambda i: (0, trail(i))) for b in blocks],
        out_shape=[jax.ShapeDtypeStruct(b.shape, BF) for b in blocks],
        scratch_shapes=[pltpu.VMEM((rows, 2 * units), F32), pltpu.VMEM((rows, units), BF)],
        compiler_params=pltpu.CompilerParams(vmem_limit_bytes=40 * 1024 * 1024),
        cost_estimate=pl.CostEstimate(flops=1, bytes_accessed=1, transcendentals=0),
        name="expert",
    )(*blocks, gate_weight, up_weight, down_weight)


def shards(
    queries,
    keys,
    values,
    segment_ids,
    residual,
    w_out,
    norm_gain,
    w_router,
    routes,
    w_gate,
    w_up,
    w_down,
):
    w_out_all = lax.all_gather(w_out, CTX, axis=1, tiled=True)
    attention = attend(queries, keys, values, segment_ids)
    head_partial = jnp.dot(attention, w_out_all, preferred_element_type=F32).astype(BF)
    width = head_partial.shape[1]
    tokens = routes.shape[0]

    route_flat = routes.reshape(-1)
    expert_ids = jnp.arange(EXPERTS, dtype=jnp.int32)
    onehot = (route_flat[:, None] == expert_ids).astype(jnp.int32)
    ranks = jnp.sum((jnp.cumsum(onehot, axis=0) - onehot) * onehot, axis=-1)
    slot_of_route = (route_flat * SLOTS + ranks).reshape(tokens, 2)
    slot_ids = jnp.arange(EXPERTS * SLOTS, dtype=jnp.int32)
    hot = slot_of_route[:, :, None] == slot_ids
    picks = jnp.any(hot, axis=1).astype(BF)
    head_partial, picks, hot = lax.optimization_barrier((head_partial, picks, hot))

    head_terms = lax.all_to_all(
        head_partial.reshape(16, tokens, width), EXP, split_axis=0, concat_axis=0, tiled=True
    )
    mixed = residual.astype(F32) + jnp.sum(head_terms.astype(F32), axis=0)
    normed = (
        mixed * lax.rsqrt(jnp.mean(mixed * mixed, axis=-1, keepdims=True) + EPSILON) * norm_gain
    ).astype(BF)

    outgoing = jnp.dot(picks.T, normed, preferred_element_type=F32).astype(BF)

    incoming = lax.all_to_all(
        outgoing.reshape(EXPERTS, SLOTS, width), "z", split_axis=0, concat_axis=0, tiled=True
    ).reshape(EXPERTS * SLOTS, width)
    slot_sums = plane_experts(
        incoming, lambda blocks: expert(blocks, w_gate[0], w_up[0], w_down[0])
    )
    logits = jnp.dot(normed, w_router, preferred_element_type=F32)
    chosen = jnp.sum((routes[..., None] == expert_ids).astype(F32) * logits[:, None, :], axis=-1)
    gates = jax.nn.softmax(chosen, axis=-1)
    slot_gates = jnp.sum(jnp.where(hot, gates[:, :, None], 0.0), axis=1)
    slot_sums, slot_gates = lax.optimization_barrier((slot_sums, slot_gates))
    returned = lax.all_to_all(
        slot_sums.reshape(EXPERTS, SLOTS, width), "z", split_axis=0, concat_axis=0, tiled=True
    ).reshape(EXPERTS * SLOTS, width)

    mixture = jnp.dot(
        slot_gates,
        returned.astype(F32),
        precision=lax.Precision.HIGHEST,
        preferred_element_type=F32,
    )
    return (mixed + mixture).astype(BF)


def solution(mesh):
    fine = Mesh(mesh.devices.reshape(4, 2, 2, 8, 2), ("x", "yl", "core", "z", "yh"))
    both = CTX + EXP
    placed = (
        P(CTX, EXP),
        P(CTX, None),
        P(CTX, None),
        P(CTX),
        P(both, None),
        P(EXP, CTX),
        P(),
        P(),
        P(both, None),
        P(EXP, None, CTX),
        P(EXP, None, CTX),
        P(EXP, CTX, None),
    )
    return jax.shard_map(
        shards, mesh=fine, in_specs=placed, out_specs=P(both, None), check_vma=False
    )
```

```python
import functools

import jax
import jax.numpy as jnp
import numpy as np
from jax import lax
from jax.experimental import pallas as pl
from jax.experimental.pallas import tpu as pltpu
from jax.sharding import Mesh, PartitionSpec as P

HEADS = 48
KVH = 8
HD = 128
EXPERTS = 8
NEG_FILL = -1e30
EPSILON = 1e-05
SLOTS = 3

CTX, EXP, PLANE = ("x", "yl", "core"), ("z", "yh"), ("x", "yl", "core", "yh")
BF, F32 = jnp.bfloat16, jnp.float32


def swap(value, axis):
    return lax.ppermute(value, axis, [(0, 1), (1, 0)])


def plane_shift(value, by, turn):
    def index(x, y, core):
        return ((x * 2 + y % 2) * 2 + core) * 2 + y // 2

    pairs = [
        (
            index(x, y, core),
            index((x + by) % 4, y, core) if core == turn else index(x, (y + by) % 4, core),
        )
        for x in range(4)
        for y in range(4)
        for core in (0, 1)
    ]
    return lax.ppermute(value, PLANE, pairs)


def total(first, *others):
    result = first.astype(F32)
    for other in others:
        result = result + other.astype(F32)
    return result


def attend(queries, keys, values, segment_ids):
    z = lax.axis_index("z")
    rows = queries.shape[0]
    seg_row = jnp.pad(segment_ids.astype(BF)[None, :], ((0, 7), (0, rows)))
    block = jnp.concatenate(
        [
            jnp.concatenate(
                [
                    lax.dynamic_slice_in_dim(keys, z * HD, HD, 1),
                    lax.dynamic_slice_in_dim(values, z * HD, HD, 1),
                ],
                axis=1,
            ),
            seg_row,
        ],
        axis=0,
    )
    x, yl, core = lax.axis_index("x"), lax.axis_index("yl"), lax.axis_index("core")
    along_x = [lax.ppermute(block, "x", [(i, (i + by) % 4) for i in range(4)]) for by in (1, 3, 2)]
    blocks = jnp.stack([block] + along_x)
    blocks = jnp.stack([blocks, swap(blocks, "yl")])
    blocks = jnp.stack([blocks, swap(blocks, "core")])
    places = [
        ((x + dx) & 3) * 4 + ((yl + dy) & 1) * 2 + ((core + dc) & 1)
        for dc in (0, 1)
        for dy in (0, 1)
        for dx in (0, 3, 1, 2)
    ]
    blocks = blocks.reshape(16, rows + 8, 2 * HD)
    key_rows = blocks[:, :rows, :HD].reshape(16 * rows, HD)
    value_rows = blocks[:, :rows, HD:].reshape(16 * rows, HD)
    seg_keys = blocks[:, rows, :rows].reshape(16 * rows).astype(jnp.int32)
    row_ids = jnp.arange(rows, dtype=jnp.int32)
    key_pos = (jnp.stack(places)[:, None] * rows + row_ids[None, :]).reshape(16 * rows)
    query_pos = (x * 4 + yl * 2 + core) * rows + row_ids
    allowed = (key_pos[None, :] <= query_pos[:, None]) & (
        seg_keys[None, :] == segment_ids[:, None]
    )
    head_count = queries.shape[1] // HD
    query_heads = queries.reshape(rows, head_count, HD)
    scores = jnp.einsum("qrd,kd->rqk", query_heads, key_rows, preferred_element_type=F32)
    scores = jnp.where(allowed[None], scores * HD ** (-0.5), NEG_FILL)
    peak = jnp.max(scores, axis=-1, keepdims=True)
    weights = jnp.where(allowed[None], jnp.exp(scores - peak), 0.0)
    sums = jnp.sum(weights, axis=-1)
    update = jnp.einsum(
        "rqk,kd->rqd", weights.astype(BF), value_rows, preferred_element_type=F32
    )
    attention = (update / sums[..., None]).astype(BF)
    return attention.transpose(1, 0, 2).reshape(rows, head_count * HD)


def gather_plane(rows):
    near = [plane_shift(rows, by, 0) for by in (1, -1, 2)]
    rows = jnp.concatenate([rows] + near)
    half = rows.shape[0] // 2
    left, right = plane_shift(rows, 1, 1), plane_shift(rows, -1, 1)
    far_first = plane_shift(left[:half], 1, 1)
    far_second = plane_shift(right[half:], -1, 1)
    mine = [rows, left, right, far_first, far_second]
    return mine, [swap(block, "core") for block in mine]


def scatter_plane(mine, other):
    far_first, far_second = [total(mine[i], swap(other[i], "core")).astype(BF) for i in (5, 6)]
    left_second, right_first = [total(mine[i], swap(other[i], "core")).astype(BF) for i in (2, 3)]
    far_first, far_second, left_second, right_first = lax.optimization_barrier(
        (far_first, far_second, left_second, right_first)
    )
    far_first, far_second = plane_shift(far_first, -1, 1), plane_shift(far_second, 1, 1)
    left_second, right_first = plane_shift(left_second, -1, 1), plane_shift(right_first, 1, 1)
    left_first, right_second = [total(mine[i], swap(other[i], "core")) for i in (1, 4)]
    left_first = plane_shift((left_first + far_first.astype(F32)).astype(BF), -1, 1)
    right_second = plane_shift((right_second + far_second.astype(F32)).astype(BF), 1, 1)
    own_other = swap(lax.optimization_barrier((other[0], far_first))[0], "core")
    half = left_second.shape[0]
    first = total(mine[0][:half], own_other[:half], left_first, right_first)
    second = total(mine[0][half:], own_other[half:], left_second, right_second)
    first, second = [value.astype(BF).reshape(2, half // 2, -1) for value in (first, second)]
    sent = ((first[1], -1), (second[0], 1), (second[1], 2))
    return total(first[0], *[plane_shift(block, by, 0) for block, by in sent]).astype(BF)


STEPS = 2


def expert_kernel(count, *refs):
    rows_in, (gate_ref, up_ref, down_ref) = refs[:count], refs[count : count + 3]
    rows_out, (sums, hidden) = refs[count + 3 : -2], refs[-2:]
    step = pl.program_id(0)
    units = gate_ref.shape[1]

    def add(fresh):
        rows = jnp.concatenate([block[...] for block in rows_in])
        gate_val = jnp.dot(rows, gate_ref[...], preferred_element_type=F32)
        up_val = jnp.dot(rows, up_ref[...], preferred_element_type=F32)
        if fresh:
            sums[:, :units] = gate_val
            sums[:, units:] = up_val
        else:
            sums[:, :units] += gate_val
            sums[:, units:] += up_val

    pl.when(step == 0)(lambda: add(True))
    pl.when((step > 0) & (step < STEPS))(lambda: add(False))

    @pl.when(step == STEPS - 1)
    def _():
        gate_val, up_val = sums[:, :units], sums[:, units:]
        hidden[...] = (gate_val / (1.0 + jnp.exp(-gate_val)) * up_val).astype(BF)

    @pl.when(step >= STEPS)
    def _():
        result = jnp.dot(hidden[...], down_ref[...], preferred_element_type=F32).astype(BF)
        first = 0
        for block in rows_out:
            block[...] = result[first : first + block.shape[0]]
            first += block.shape[0]


def expert(blocks, sizes, gate_weight, up_weight, down_weight):
    features, units = gate_weight.shape
    rows = sum(block.shape[0] for block in blocks)
    wide = features // STEPS
    lead, trail = lambda i: jnp.minimum(i, STEPS - 1), lambda i: jnp.maximum(i - STEPS, 0)
    weight_in = pl.BlockSpec((wide, units), lambda i: (lead(i), 0))
    weight_out = pl.BlockSpec((units, wide), lambda i: (0, trail(i)))
    return pl.pallas_call(
        functools.partial(expert_kernel, len(blocks)),
        grid=(2 * STEPS,),
        in_specs=[pl.BlockSpec((b.shape[0], wide), lambda i: (0, lead(i))) for b in blocks]
        + [weight_in, weight_in, weight_out],
        out_specs=[pl.BlockSpec((size, wide), lambda i: (0, trail(i))) for size in sizes],
        out_shape=[jax.ShapeDtypeStruct((size, features), BF) for size in sizes],
        scratch_shapes=[pltpu.VMEM((rows, 2 * units), F32), pltpu.VMEM((rows, units), BF)],
        compiler_params=pltpu.CompilerParams(vmem_limit_bytes=40 * 1024 * 1024),
        cost_estimate=pl.CostEstimate(
            flops=6 * rows * features * units,
            bytes_accessed=2 * (3 * features * units + 2 * rows * features),
            transcendentals=rows * units,
        ),
        name="expert",
    )(*blocks, gate_weight, up_weight, down_weight)


def shards(
    queries,
    keys,
    values,
    segment_ids,
    residual,
    w_out,
    norm_gain,
    w_router,
    routes,
    w_gate,
    w_up,
    w_down,
):
    w_out_all = lax.all_gather(w_out, CTX, axis=1, tiled=True)
    attention = attend(queries, keys, values, segment_ids)
    head_partial = jnp.dot(attention, w_out_all, preferred_element_type=F32).astype(BF)
    width = head_partial.shape[1]
    tokens = routes.shape[0]

    route_flat = routes.reshape(-1)
    expert_ids = jnp.arange(EXPERTS, dtype=jnp.int32)
    onehot = (route_flat[:, None] == expert_ids).astype(jnp.int32)
    ranks = jnp.sum((jnp.cumsum(onehot, axis=0) - onehot) * onehot, axis=-1)
    slot_of_route = (route_flat * SLOTS + ranks).reshape(tokens, 2)
    slot_ids = jnp.arange(EXPERTS * SLOTS, dtype=jnp.int32)
    hot = slot_of_route[:, :, None] == slot_ids
    picks = jnp.any(hot, axis=1).astype(BF)
    head_partial, picks, hot = lax.optimization_barrier((head_partial, picks, hot))

    head_terms = lax.all_to_all(
        head_partial.reshape(16, tokens, width), EXP, split_axis=0, concat_axis=0, tiled=True
    )
    mixed = residual.astype(F32) + jnp.sum(head_terms.astype(F32), axis=0)
    normed = (
        mixed * lax.rsqrt(jnp.mean(mixed * mixed, axis=-1, keepdims=True) + EPSILON) * norm_gain
    ).astype(BF)

    outgoing = jnp.dot(picks.T, normed, preferred_element_type=F32).astype(BF)

    incoming = lax.all_to_all(
        outgoing.reshape(EXPERTS, SLOTS, width), "z", split_axis=0, concat_axis=0, tiled=True
    ).reshape(EXPERTS * SLOTS, width)
    mine, other = gather_plane(incoming)
    weights = w_gate[0], w_up[0], w_down[0]
    half = mine[0].shape[0] // 2
    sizes = (2 * half,) + (half,) * 6
    slot_sums = scatter_plane(expert(mine, sizes, *weights), expert(other, sizes, *weights))
    logits = jnp.dot(normed, w_router, preferred_element_type=F32)
    chosen = jnp.sum((routes[..., None] == expert_ids).astype(F32) * logits[:, None, :], axis=-1)
    gates = jax.nn.softmax(chosen, axis=-1)
    slot_gates = jnp.sum(jnp.where(hot, gates[:, :, None], 0.0), axis=1)
    slot_sums, slot_gates = lax.optimization_barrier((slot_sums, slot_gates))
    returned = lax.all_to_all(
        slot_sums.reshape(EXPERTS, SLOTS, width), "z", split_axis=0, concat_axis=0, tiled=True
    ).reshape(EXPERTS * SLOTS, width)

    mixture = jnp.dot(
        slot_gates,
        returned.astype(F32),
        precision=lax.Precision.HIGHEST,
        preferred_element_type=F32,
    )
    return (mixed + mixture).astype(BF)


def solution(mesh):
    fine = Mesh(mesh.devices.reshape(4, 2, 2, 8, 2), ("x", "yl", "core", "z", "yh"))
    both = CTX + EXP
    placed = (
        P(CTX, EXP),
        P(CTX, None),
        P(CTX, None),
        P(CTX),
        P(both, None),
        P(EXP, CTX),
        P(),
        P(),
        P(both, None),
        P(EXP, None, CTX),
        P(EXP, None, CTX),
        P(EXP, CTX, None),
    )
    return jax.shard_map(
        shards, mesh=fine, in_specs=placed, out_specs=P(both, None), check_vma=False
    )
```

```python
import functools

import jax
import jax.numpy as jnp
import numpy as np
from jax import lax
from jax.experimental import pallas as pl
from jax.experimental.pallas import tpu as pltpu
from jax.sharding import Mesh, PartitionSpec as P

HEADS = 48
KVH = 8
HD = 128
EXPERTS = 8
NEG_FILL = -1e30
EPSILON = 1e-05
SLOTS = 3

CTX, EXP, PLANE = ("x", "yl", "core"), ("z", "yh"), ("x", "yl", "core", "yh")
BF, F32 = jnp.bfloat16, jnp.float32


def swap(value, axis):
    return lax.ppermute(value, axis, [(0, 1), (1, 0)])


def plane_shift(value, by, turn):
    def index(x, y, core):
        return ((x * 2 + y % 2) * 2 + core) * 2 + y // 2

    pairs = [
        (
            index(x, y, core),
            index((x + by) % 4, y, core) if core == turn else index(x, (y + by) % 4, core),
        )
        for x in range(4)
        for y in range(4)
        for core in (0, 1)
    ]
    return lax.ppermute(value, PLANE, pairs)


def total(first, *others):
    result = first.astype(F32)
    for other in others:
        result = result + other.astype(F32)
    return result


def attend(queries, keys, values, segment_ids):
    z = lax.axis_index("z")
    rows = queries.shape[0]
    seg_row = jnp.pad(segment_ids.astype(BF)[None, :], ((0, 7), (0, rows)))
    block = jnp.concatenate(
        [
            jnp.concatenate(
                [
                    lax.dynamic_slice_in_dim(keys, z * HD, HD, 1),
                    lax.dynamic_slice_in_dim(values, z * HD, HD, 1),
                ],
                axis=1,
            ),
            seg_row,
        ],
        axis=0,
    )
    x, yl, core = lax.axis_index("x"), lax.axis_index("yl"), lax.axis_index("core")
    along_x = [lax.ppermute(block, "x", [(i, (i + by) % 4) for i in range(4)]) for by in (1, 3, 2)]
    blocks = jnp.stack([block] + along_x)
    blocks = jnp.stack([blocks, swap(blocks, "yl")])
    blocks = jnp.stack([blocks, swap(blocks, "core")])
    places = [
        ((x + dx) & 3) * 4 + ((yl + dy) & 1) * 2 + ((core + dc) & 1)
        for dc in (0, 1)
        for dy in (0, 1)
        for dx in (0, 3, 1, 2)
    ]
    blocks = blocks.reshape(16, rows + 8, 2 * HD)
    key_rows = blocks[:, :rows, :HD].reshape(16 * rows, HD)
    value_rows = blocks[:, :rows, HD:].reshape(16 * rows, HD)
    seg_keys = blocks[:, rows, :rows].reshape(16 * rows).astype(jnp.int32)
    row_ids = jnp.arange(rows, dtype=jnp.int32)
    key_pos = (jnp.stack(places)[:, None] * rows + row_ids[None, :]).reshape(16 * rows)
    query_pos = (x * 4 + yl * 2 + core) * rows + row_ids
    allowed = (key_pos[None, :] <= query_pos[:, None]) & (
        seg_keys[None, :] == segment_ids[:, None]
    )
    head_count = queries.shape[1] // HD
    query_heads = queries.reshape(rows, head_count, HD)
    scores = jnp.einsum("qrd,kd->rqk", query_heads, key_rows, preferred_element_type=F32)
    scores = jnp.where(allowed[None], scores * HD ** (-0.5), NEG_FILL)
    peak = jnp.max(scores, axis=-1, keepdims=True)
    weights = jnp.where(allowed[None], jnp.exp(scores - peak), 0.0)
    sums = jnp.sum(weights, axis=-1)
    update = jnp.einsum(
        "rqk,kd->rqd", weights.astype(BF), value_rows, preferred_element_type=F32
    )
    attention = (update / sums[..., None]).astype(BF)
    return attention.transpose(1, 0, 2).reshape(rows, head_count * HD)


def plane_experts(rows, expert_of):
    near = [plane_shift(rows, by, 0) for by in (1, -1, 2)]
    rows = jnp.concatenate([rows] + near)
    half = rows.shape[0] // 2
    left, right = plane_shift(rows, 1, 1), plane_shift(rows, -1, 1)
    far_first = plane_shift(left[:half], 1, 1)
    far_second = plane_shift(right[half:], -1, 1)
    mine = [rows, left, right]
    other = [swap(block, "core") for block in mine]
    near = expert_of(mine)
    far_first, far_second, first = lax.optimization_barrier((far_first, far_second, near[0]))
    far = [far_first, far_second]
    rest = expert_of(far + other + [swap(block, "core") for block in far])
    return [first, *near[1:], *rest[:2]], rest[2:]


def scatter_plane(mine, other):
    far_first, far_second = [total(mine[i], swap(other[i], "core")).astype(BF) for i in (3, 4)]
    far_first, far_second = lax.optimization_barrier((far_first, far_second))
    half = far_first.shape[0]
    far_first, far_second = plane_shift(far_first, -1, 1), plane_shift(far_second, 1, 1)
    left = total(mine[1], swap(other[1], "core"), jnp.pad(far_first, ((0, half), (0, 0))))
    right = total(mine[2], swap(other[2], "core"), jnp.pad(far_second, ((half, 0), (0, 0))))
    left, right = left.astype(BF), right.astype(BF)
    left, right = lax.optimization_barrier((left, right))
    left, right = plane_shift(left, -1, 1), plane_shift(right, 1, 1)
    rows = total(mine[0], swap(other[0], "core"), left, right).astype(BF)
    rows = rows.reshape(4, -1, rows.shape[-1])
    near = [plane_shift(rows[i], by, 0) for i, by in ((1, -1), (2, 1), (3, 2))]
    return total(rows[0], *near).astype(BF)


STEPS = 2


def expert_kernel(count, *refs):
    rows_in, (gate_ref, up_ref, down_ref) = refs[:count], refs[count : count + 3]
    rows_out, (sums, hidden) = refs[count + 3 : 2 * count + 3], refs[2 * count + 3 :]
    step = pl.program_id(0)
    units = gate_ref.shape[1]

    def add(fresh):
        rows = jnp.concatenate([block[...] for block in rows_in])
        gate_val = jnp.dot(rows, gate_ref[...], preferred_element_type=F32)
        up_val = jnp.dot(rows, up_ref[...], preferred_element_type=F32)
        if fresh:
            sums[:, :units] = gate_val
            sums[:, units:] = up_val
        else:
            sums[:, :units] += gate_val
            sums[:, units:] += up_val

    pl.when(step == 0)(lambda: add(True))
    pl.when((step > 0) & (step < STEPS))(lambda: add(False))

    @pl.when(step == STEPS - 1)
    def _():
        gate_val, up_val = sums[:, :units], sums[:, units:]
        hidden[...] = (gate_val / (1.0 + jnp.exp(-gate_val)) * up_val).astype(BF)

    @pl.when(step >= STEPS)
    def _():
        result = jnp.dot(hidden[...], down_ref[...], preferred_element_type=F32).astype(BF)
        first = 0
        for block in rows_out:
            block[...] = result[first : first + block.shape[0]]
            first += block.shape[0]


def expert(blocks, gate_weight, up_weight, down_weight):
    features, units = gate_weight.shape
    rows = sum(block.shape[0] for block in blocks)
    wide = features // STEPS
    lead, trail = lambda i: jnp.minimum(i, STEPS - 1), lambda i: jnp.maximum(i - STEPS, 0)
    weight_in = pl.BlockSpec((wide, units), lambda i: (lead(i), 0))
    weight_out = pl.BlockSpec((units, wide), lambda i: (0, trail(i)))
    return pl.pallas_call(
        functools.partial(expert_kernel, len(blocks)),
        grid=(2 * STEPS,),
        in_specs=[pl.BlockSpec((b.shape[0], wide), lambda i: (0, lead(i))) for b in blocks]
        + [weight_in, weight_in, weight_out],
        out_specs=[pl.BlockSpec((b.shape[0], wide), lambda i: (0, trail(i))) for b in blocks],
        out_shape=[jax.ShapeDtypeStruct(b.shape, BF) for b in blocks],
        scratch_shapes=[pltpu.VMEM((rows, 2 * units), F32), pltpu.VMEM((rows, units), BF)],
        compiler_params=pltpu.CompilerParams(vmem_limit_bytes=40 * 1024 * 1024),
        cost_estimate=pl.CostEstimate(
            flops=6 * rows * features * units,
            bytes_accessed=2 * (3 * features * units + 2 * rows * features),
            transcendentals=rows * units,
        ),
        name="expert",
    )(*blocks, gate_weight, up_weight, down_weight)


def shards(
    queries,
    keys,
    values,
    segment_ids,
    residual,
    w_out,
    norm_gain,
    w_router,
    routes,
    w_gate,
    w_up,
    w_down,
):
    w_out_all = lax.all_gather(w_out, CTX, axis=1, tiled=True)
    attention = attend(queries, keys, values, segment_ids)
    head_partial = jnp.dot(attention, w_out_all, preferred_element_type=F32).astype(BF)
    width = head_partial.shape[1]
    tokens = routes.shape[0]

    route_flat = routes.reshape(-1)
    expert_ids = jnp.arange(EXPERTS, dtype=jnp.int32)
    onehot = (route_flat[:, None] == expert_ids).astype(jnp.int32)
    ranks = jnp.sum((jnp.cumsum(onehot, axis=0) - onehot) * onehot, axis=-1)
    slot_of_route = (route_flat * SLOTS + ranks).reshape(tokens, 2)
    slot_ids = jnp.arange(EXPERTS * SLOTS, dtype=jnp.int32)
    hot = slot_of_route[:, :, None] == slot_ids
    picks = jnp.any(hot, axis=1).astype(BF)
    yh = lax.axis_index("yh")
    head_partial, picks, hot, yh = lax.optimization_barrier((head_partial, picks, hot, yh))

    head_terms = lax.all_to_all(
        head_partial.reshape(8, 2 * tokens, width), "z", split_axis=0, concat_axis=0, tiled=True
    )
    head_sums = jnp.sum(head_terms.astype(F32), axis=0).reshape(2, tokens, width)
    own_sum = lax.dynamic_index_in_dim(head_sums, yh, 0, keepdims=False)
    sent = lax.dynamic_index_in_dim(head_sums, 1 - yh, 0, keepdims=False).astype(BF)
    mixed = residual.astype(F32) + own_sum + swap(sent, "yh").astype(F32)
    normed = (
        mixed * lax.rsqrt(jnp.mean(mixed * mixed, axis=-1, keepdims=True) + EPSILON) * norm_gain
    ).astype(BF)

    outgoing = jnp.dot(picks.T, normed, preferred_element_type=F32).astype(BF)

    incoming = lax.all_to_all(
        outgoing.reshape(EXPERTS, SLOTS, width), "z", split_axis=0, concat_axis=0, tiled=True
    ).reshape(EXPERTS * SLOTS, width)
    weights = w_gate[0], w_up[0], w_down[0]
    mine, other = plane_experts(incoming, lambda blocks: expert(blocks, *weights))
    slot_sums = scatter_plane(mine, other)
    logits = jnp.dot(normed, w_router, preferred_element_type=F32)
    chosen = jnp.sum((routes[..., None] == expert_ids).astype(F32) * logits[:, None, :], axis=-1)
    gates = jax.nn.softmax(chosen, axis=-1)
    slot_gates = jnp.sum(jnp.where(hot, gates[:, :, None], 0.0), axis=1)
    slot_sums, slot_gates = lax.optimization_barrier((slot_sums, slot_gates))
    returned = lax.all_to_all(
        slot_sums.reshape(EXPERTS, SLOTS, width), "z", split_axis=0, concat_axis=0, tiled=True
    ).reshape(EXPERTS * SLOTS, width)

    mixture = jnp.dot(
        slot_gates,
        returned.astype(F32),
        precision=lax.Precision.HIGHEST,
        preferred_element_type=F32,
    )
    return (mixed + mixture).astype(BF)


def solution(mesh):
    fine = Mesh(mesh.devices.reshape(4, 2, 2, 8, 2), ("x", "yl", "core", "z", "yh"))
    both = CTX + EXP
    placed = (
        P(CTX, EXP),
        P(CTX, None),
        P(CTX, None),
        P(CTX),
        P(both, None),
        P(EXP, CTX),
        P(),
        P(),
        P(both, None),
        P(EXP, None, CTX),
        P(EXP, None, CTX),
        P(EXP, CTX, None),
    )
    return jax.shard_map(
        shards, mesh=fine, in_specs=placed, out_specs=P(both, None), check_vma=False
    )
```

```python
import functools

import jax
import jax.numpy as jnp
import numpy as np
from jax import lax
from jax.experimental import pallas as pl
from jax.experimental.pallas import tpu as pltpu
from jax.sharding import Mesh, PartitionSpec as P

HEADS = 48
KVH = 8
HD = 128
EXPERTS = 8
NEG_FILL = -1e30
EPSILON = 1e-05
SLOTS = 3

CTX, EXP, PLANE = ("x", "yl", "core"), ("z", "yh"), ("x", "yl", "core", "yh")
BF, F32 = jnp.bfloat16, jnp.float32


def swap(value, axis):
    return lax.ppermute(value, axis, [(0, 1), (1, 0)])


def plane_shift(value, by, turn):
    def index(x, y, core):
        return ((x * 2 + y % 2) * 2 + core) * 2 + y // 2

    pairs = [
        (
            index(x, y, core),
            index((x + by) % 4, y, core) if core == turn else index(x, (y + by) % 4, core),
        )
        for x in range(4)
        for y in range(4)
        for core in (0, 1)
    ]
    return lax.ppermute(value, PLANE, pairs)


def total(first, *others):
    result = first.astype(F32)
    for other in others:
        result = result + other.astype(F32)
    return result


def attend(queries, keys, values, segment_ids):
    z = lax.axis_index("z")
    rows = queries.shape[0]
    seg_row = jnp.pad(segment_ids.astype(BF)[None, :], ((0, 7), (0, rows)))
    block = jnp.concatenate(
        [
            jnp.concatenate(
                [
                    lax.dynamic_slice_in_dim(keys, z * HD, HD, 1),
                    lax.dynamic_slice_in_dim(values, z * HD, HD, 1),
                ],
                axis=1,
            ),
            seg_row,
        ],
        axis=0,
    )
    x, yl, core = lax.axis_index("x"), lax.axis_index("yl"), lax.axis_index("core")
    along_x = [lax.ppermute(block, "x", [(i, (i + by) % 4) for i in range(4)]) for by in (1, 3, 2)]
    blocks = jnp.stack([block] + along_x)
    blocks = jnp.stack([blocks, swap(blocks, "yl")])
    blocks = jnp.stack([blocks, swap(blocks, "core")])
    places = [
        ((x + dx) & 3) * 4 + ((yl + dy) & 1) * 2 + ((core + dc) & 1)
        for dc in (0, 1)
        for dy in (0, 1)
        for dx in (0, 3, 1, 2)
    ]
    blocks = blocks.reshape(16, rows + 8, 2 * HD)
    key_rows = blocks[:, :rows, :HD].reshape(16 * rows, HD)
    value_rows = blocks[:, :rows, HD:].reshape(16 * rows, HD)
    seg_keys = blocks[:, rows, :rows].reshape(16 * rows).astype(jnp.int32)
    row_ids = jnp.arange(rows, dtype=jnp.int32)
    key_pos = (jnp.stack(places)[:, None] * rows + row_ids[None, :]).reshape(16 * rows)
    query_pos = (x * 4 + yl * 2 + core) * rows + row_ids
    allowed = (key_pos[None, :] <= query_pos[:, None]) & (
        seg_keys[None, :] == segment_ids[:, None]
    )
    head_count = queries.shape[1] // HD
    query_heads = queries.reshape(rows, head_count, HD)
    scores = jnp.einsum("qrd,kd->rqk", query_heads, key_rows, preferred_element_type=F32)
    scores = jnp.where(allowed[None], scores * HD ** (-0.5), NEG_FILL)
    peak = jnp.max(scores, axis=-1, keepdims=True)
    weights = jnp.where(allowed[None], jnp.exp(scores - peak), 0.0)
    sums = jnp.sum(weights, axis=-1)
    update = jnp.einsum(
        "rqk,kd->rqd", weights.astype(BF), value_rows, preferred_element_type=F32
    )
    attention = (update / sums[..., None]).astype(BF)
    return attention.transpose(1, 0, 2).reshape(rows, head_count * HD)


def gather_plane(rows):
    near = [plane_shift(rows, by, 0) for by in (1, -1, 2)]
    rows = jnp.concatenate([rows] + near)
    half = rows.shape[0] // 2
    left, right = plane_shift(rows, 1, 1), plane_shift(rows, -1, 1)
    far_first = plane_shift(left[:half], 1, 1)
    far_second = plane_shift(right[half:], -1, 1)
    mine = [rows, left, right, far_first, far_second]
    return mine, [swap(block, "core") for block in mine]


def scatter_plane(mine, other):
    far_first, far_second = [total(mine[i], swap(other[i], "core")).astype(BF) for i in (3, 4)]
    far_first, far_second = lax.optimization_barrier((far_first, far_second))
    half = far_first.shape[0]
    far_first, far_second = plane_shift(far_first, -1, 1), plane_shift(far_second, 1, 1)
    left = total(mine[1], swap(other[1], "core"), jnp.pad(far_first, ((0, half), (0, 0))))
    right = total(mine[2], swap(other[2], "core"), jnp.pad(far_second, ((half, 0), (0, 0))))
    left, right = left.astype(BF), right.astype(BF)
    left, right = lax.optimization_barrier((left, right))
    left, right = plane_shift(left, -1, 1), plane_shift(right, 1, 1)
    rows = total(mine[0], swap(other[0], "core"), left, right).astype(BF)
    rows = rows.reshape(4, -1, rows.shape[-1])
    near = [plane_shift(rows[i], by, 0) for i, by in ((1, -1), (2, 1), (3, 2))]
    return total(rows[0], *near).astype(BF)


STEPS = 2


def expert_kernel(count, *refs):
    rows_in, (gate_ref, up_ref, down_ref) = refs[:count], refs[count : count + 3]
    rows_out, (sums, hidden) = refs[count + 3 : 2 * count + 3], refs[2 * count + 3 :]
    step = pl.program_id(0)
    units = gate_ref.shape[1]

    def add(fresh):
        rows = jnp.concatenate([block[...] for block in rows_in])
        gate_val = jnp.dot(rows, gate_ref[...], preferred_element_type=F32)
        up_val = jnp.dot(rows, up_ref[...], preferred_element_type=F32)
        if fresh:
            sums[:, :units] = gate_val
            sums[:, units:] = up_val
        else:
            sums[:, :units] += gate_val
            sums[:, units:] += up_val

    pl.when(step == 0)(lambda: add(True))
    pl.when((step > 0) & (step < STEPS))(lambda: add(False))

    @pl.when(step == STEPS - 1)
    def _():
        gate_val, up_val = sums[:, :units], sums[:, units:]
        hidden[...] = (gate_val / (1.0 + jnp.exp(-gate_val)) * up_val).astype(BF)

    @pl.when(step >= STEPS)
    def _():
        result = jnp.dot(hidden[...], down_ref[...], preferred_element_type=F32).astype(BF)
        first = 0
        for block in rows_out:
            block[...] = result[first : first + block.shape[0]]
            first += block.shape[0]


def expert(blocks, gate_weight, up_weight, down_weight):
    features, units = gate_weight.shape
    rows = sum(block.shape[0] for block in blocks)
    wide = features // STEPS
    lead, trail = lambda i: jnp.minimum(i, STEPS - 1), lambda i: jnp.maximum(i - STEPS, 0)
    weight_in = pl.BlockSpec((wide, units), lambda i: (lead(i), 0))
    weight_out = pl.BlockSpec((units, wide), lambda i: (0, trail(i)))
    return pl.pallas_call(
        functools.partial(expert_kernel, len(blocks)),
        grid=(2 * STEPS,),
        in_specs=[pl.BlockSpec((b.shape[0], wide), lambda i: (0, lead(i))) for b in blocks]
        + [weight_in, weight_in, weight_out],
        out_specs=[pl.BlockSpec((b.shape[0], wide), lambda i: (0, trail(i))) for b in blocks],
        out_shape=[jax.ShapeDtypeStruct(b.shape, BF) for b in blocks],
        scratch_shapes=[pltpu.VMEM((rows, 2 * units), F32), pltpu.VMEM((rows, units), BF)],
        compiler_params=pltpu.CompilerParams(vmem_limit_bytes=28 * 1024 * 1024),
        cost_estimate=pl.CostEstimate(
            flops=6 * rows * features * units,
            bytes_accessed=2 * (3 * features * units + 2 * rows * features),
            transcendentals=rows * units,
        ),
        name="expert",
    )(*blocks, gate_weight, up_weight, down_weight)


def shards(
    queries,
    keys,
    values,
    segment_ids,
    residual,
    w_out,
    norm_gain,
    w_router,
    routes,
    w_gate,
    w_up,
    w_down,
):
    w_out_all = lax.all_gather(w_out, CTX, axis=1, tiled=True)
    attention = attend(queries, keys, values, segment_ids)
    head_partial = jnp.dot(attention, w_out_all, preferred_element_type=F32).astype(BF)
    width = head_partial.shape[1]
    tokens = routes.shape[0]

    route_flat = routes.reshape(-1)
    expert_ids = jnp.arange(EXPERTS, dtype=jnp.int32)
    onehot = (route_flat[:, None] == expert_ids).astype(jnp.int32)
    ranks = jnp.sum((jnp.cumsum(onehot, axis=0) - onehot) * onehot, axis=-1)
    slot_of_route = (route_flat * SLOTS + ranks).reshape(tokens, 2)
    slot_ids = jnp.arange(EXPERTS * SLOTS, dtype=jnp.int32)
    hot = slot_of_route[:, :, None] == slot_ids
    picks = jnp.any(hot, axis=1).astype(BF)
    head_partial, picks, hot = lax.optimization_barrier((head_partial, picks, hot))

    head_terms = lax.all_to_all(
        head_partial.reshape(16, tokens, width), EXP, split_axis=0, concat_axis=0, tiled=True
    )
    mixed = residual.astype(F32) + jnp.sum(head_terms.astype(F32), axis=0)
    normed = (
        mixed * lax.rsqrt(jnp.mean(mixed * mixed, axis=-1, keepdims=True) + EPSILON) * norm_gain
    ).astype(BF)

    outgoing = jnp.dot(picks.T, normed, preferred_element_type=F32).astype(BF)

    incoming = lax.all_to_all(
        outgoing.reshape(EXPERTS, SLOTS, width), "z", split_axis=0, concat_axis=0, tiled=True
    ).reshape(EXPERTS * SLOTS, width)
    mine, other = gather_plane(incoming)
    weights = w_gate[0], w_up[0], w_down[0]
    slot_sums = scatter_plane(expert(mine, *weights), expert(other, *weights))
    logits = jnp.dot(normed, w_router, preferred_element_type=F32)
    chosen = jnp.sum((routes[..., None] == expert_ids).astype(F32) * logits[:, None, :], axis=-1)
    gates = jax.nn.softmax(chosen, axis=-1)
    slot_gates = jnp.sum(jnp.where(hot, gates[:, :, None], 0.0), axis=1)
    slot_sums, slot_gates = lax.optimization_barrier((slot_sums, slot_gates))
    returned = lax.all_to_all(
        slot_sums.reshape(EXPERTS, SLOTS, width), "z", split_axis=0, concat_axis=0, tiled=True
    ).reshape(EXPERTS * SLOTS, width)

    mixture = jnp.dot(
        slot_gates,
        returned.astype(F32),
        precision=lax.Precision.HIGHEST,
        preferred_element_type=F32,
    )
    return (mixed + mixture).astype(BF)


def solution(mesh):
    fine = Mesh(mesh.devices.reshape(4, 2, 2, 8, 2), ("x", "yl", "core", "z", "yh"))
    both = CTX + EXP
    placed = (
        P(CTX, EXP),
        P(CTX, None),
        P(CTX, None),
        P(CTX),
        P(both, None),
        P(EXP, CTX),
        P(),
        P(),
        P(both, None),
        P(EXP, None, CTX),
        P(EXP, None, CTX),
        P(EXP, CTX, None),
    )
    return jax.shard_map(
        shards, mesh=fine, in_specs=placed, out_specs=P(both, None), check_vma=False
    )
```

```python
import functools

import jax
import jax.numpy as jnp
import numpy as np
from jax import lax
from jax.experimental import pallas as pl
from jax.experimental.pallas import tpu as pltpu
from jax.sharding import Mesh, PartitionSpec as P

HEADS = 48
KVH = 8
HD = 128
EXPERTS = 8
NEG_FILL = -1e30
EPSILON = 1e-05
SLOTS = 3

CTX, EXP, PLANE = ("x", "yl", "core"), ("z", "yh"), ("x", "yl", "core", "yh")
BF, F32 = jnp.bfloat16, jnp.float32


def swap(value, axis):
    return lax.ppermute(value, axis, [(0, 1), (1, 0)])


def plane_shift(value, by, turn):
    def index(x, y, core):
        return ((x * 2 + y % 2) * 2 + core) * 2 + y // 2

    pairs = [
        (
            index(x, y, core),
            index((x + by) % 4, y, core) if core == turn else index(x, (y + by) % 4, core),
        )
        for x in range(4)
        for y in range(4)
        for core in (0, 1)
    ]
    return lax.ppermute(value, PLANE, pairs)


def total(first, *others):
    result = first.astype(F32)
    for other in others:
        result = result + other.astype(F32)
    return result


def attend(queries, keys, values, segment_ids):
    z = lax.axis_index("z")
    rows = queries.shape[0]
    seg_row = jnp.pad(segment_ids.astype(BF)[None, :], ((0, 7), (0, rows)))
    block = jnp.concatenate(
        [
            jnp.concatenate(
                [
                    lax.dynamic_slice_in_dim(keys, z * HD, HD, 1),
                    lax.dynamic_slice_in_dim(values, z * HD, HD, 1),
                ],
                axis=1,
            ),
            seg_row,
        ],
        axis=0,
    )
    x, yl, core = lax.axis_index("x"), lax.axis_index("yl"), lax.axis_index("core")
    along_x = [lax.ppermute(block, "x", [(i, (i + by) % 4) for i in range(4)]) for by in (1, 3, 2)]
    blocks = jnp.stack([block] + along_x)
    blocks = jnp.stack([blocks, swap(blocks, "yl")])
    blocks = jnp.stack([blocks, swap(blocks, "core")])
    places = [
        ((x + dx) & 3) * 4 + ((yl + dy) & 1) * 2 + ((core + dc) & 1)
        for dc in (0, 1)
        for dy in (0, 1)
        for dx in (0, 3, 1, 2)
    ]
    blocks = blocks.reshape(16, rows + 8, 2 * HD)
    key_rows = blocks[:, :rows, :HD].reshape(16 * rows, HD)
    value_rows = blocks[:, :rows, HD:].reshape(16 * rows, HD)
    seg_keys = blocks[:, rows, :rows].reshape(16 * rows).astype(jnp.int32)
    row_ids = jnp.arange(rows, dtype=jnp.int32)
    key_pos = (jnp.stack(places)[:, None] * rows + row_ids[None, :]).reshape(16 * rows)
    query_pos = (x * 4 + yl * 2 + core) * rows + row_ids
    allowed = (key_pos[None, :] <= query_pos[:, None]) & (
        seg_keys[None, :] == segment_ids[:, None]
    )
    head_count = queries.shape[1] // HD
    query_heads = queries.reshape(rows, head_count, HD)
    scores = jnp.einsum("qrd,kd->rqk", query_heads, key_rows, preferred_element_type=F32)
    scores = jnp.where(allowed[None], scores * HD ** (-0.5), NEG_FILL)
    peak = jnp.max(scores, axis=-1, keepdims=True)
    weights = jnp.where(allowed[None], jnp.exp(scores - peak), 0.0)
    sums = jnp.sum(weights, axis=-1)
    update = jnp.einsum(
        "rqk,kd->rqd", weights.astype(BF), value_rows, preferred_element_type=F32
    )
    attention = (update / sums[..., None]).astype(BF)
    return attention.transpose(1, 0, 2).reshape(rows, head_count * HD)


def plane_experts(rows, expert_of):
    near = [plane_shift(rows, by, 0) for by in (1, -1, 2)]
    rows = jnp.concatenate([rows] + near)
    half = rows.shape[0] // 2
    left, right = plane_shift(rows, 1, 1), plane_shift(rows, -1, 1)
    far_first = plane_shift(left[:half], 1, 1)
    far_second = plane_shift(right[half:], -1, 1)
    mine = [rows, left, right]
    other = [swap(block, "core") for block in mine]
    near = expert_of(mine)
    far_first, far_second, first = lax.optimization_barrier((far_first, far_second, near[0]))
    other = expert_of(other + [swap(far_first, "core"), swap(far_second, "core")])
    far_first, last = lax.optimization_barrier((far_first, other[4]))
    far = expert_of([far_first, far_second])
    return [first, *near[1:], *far], [*other[:4], last]


def scatter_plane(mine, other):
    far_first, far_second = [total(mine[i], swap(other[i], "core")).astype(BF) for i in (3, 4)]
    far_first, far_second = lax.optimization_barrier((far_first, far_second))
    half = far_first.shape[0]
    far_first, far_second = plane_shift(far_first, -1, 1), plane_shift(far_second, 1, 1)
    left, right = [total(mine[i], swap(other[i], "core")) for i in (1, 2)]
    left = jnp.concatenate([left[:half] + far_first.astype(F32), left[half:]]).astype(BF)
    right = jnp.concatenate([right[:half], right[half:] + far_second.astype(F32)]).astype(BF)
    left, right = lax.optimization_barrier((left, right))
    left, right = plane_shift(left, -1, 1), plane_shift(right, 1, 1)
    rows = total(mine[0], swap(other[0], "core"), left, right).astype(BF)
    rows = rows.reshape(4, -1, rows.shape[-1])
    near = [plane_shift(rows[i], by, 0) for i, by in ((1, -1), (2, 1), (3, 2))]
    return total(rows[0], *near).astype(BF)


STEPS = 2


def expert_kernel(count, *refs):
    rows_in, (gate_ref, up_ref, down_ref) = refs[:count], refs[count : count + 3]
    rows_out, (sums, hidden) = refs[count + 3 : 2 * count + 3], refs[2 * count + 3 :]
    step = pl.program_id(0)
    units = gate_ref.shape[1]

    def add(fresh):
        rows = jnp.concatenate([block[...] for block in rows_in])
        gate_val = jnp.dot(rows, gate_ref[...], preferred_element_type=F32)
        up_val = jnp.dot(rows, up_ref[...], preferred_element_type=F32)
        if fresh:
            sums[:, :units] = gate_val
            sums[:, units:] = up_val
        else:
            sums[:, :units] += gate_val
            sums[:, units:] += up_val

    pl.when(step == 0)(lambda: add(True))
    pl.when((step > 0) & (step < STEPS))(lambda: add(False))

    @pl.when(step == STEPS - 1)
    def _():
        gate_val, up_val = sums[:, :units], sums[:, units:]
        hidden[...] = (gate_val / (1.0 + jnp.exp(-gate_val)) * up_val).astype(BF)

    @pl.when(step >= STEPS)
    def _():
        result = jnp.dot(hidden[...], down_ref[...], preferred_element_type=F32).astype(BF)
        first = 0
        for block in rows_out:
            block[...] = result[first : first + block.shape[0]]
            first += block.shape[0]


def expert(blocks, gate_weight, up_weight, down_weight):
    features, units = gate_weight.shape
    rows = sum(block.shape[0] for block in blocks)
    wide = features // STEPS
    lead, trail = lambda i: jnp.minimum(i, STEPS - 1), lambda i: jnp.maximum(i - STEPS, 0)
    weight_in = pl.BlockSpec((wide, units), lambda i: (lead(i), 0))
    weight_out = pl.BlockSpec((units, wide), lambda i: (0, trail(i)))
    return pl.pallas_call(
        functools.partial(expert_kernel, len(blocks)),
        grid=(2 * STEPS,),
        in_specs=[pl.BlockSpec((b.shape[0], wide), lambda i: (0, lead(i))) for b in blocks]
        + [weight_in, weight_in, weight_out],
        out_specs=[pl.BlockSpec((b.shape[0], wide), lambda i: (0, trail(i))) for b in blocks],
        out_shape=[jax.ShapeDtypeStruct(b.shape, BF) for b in blocks],
        scratch_shapes=[pltpu.VMEM((rows, 2 * units), F32), pltpu.VMEM((rows, units), BF)],
        compiler_params=pltpu.CompilerParams(vmem_limit_bytes=30 * 1024 * 1024),
        cost_estimate=pl.CostEstimate(
            flops=6 * rows * features * units,
            bytes_accessed=2 * (3 * features * units + 2 * rows * features),
            transcendentals=rows * units,
        ),
        name="expert",
    )(*blocks, gate_weight, up_weight, down_weight)


def shards(
    queries,
    keys,
    values,
    segment_ids,
    residual,
    w_out,
    norm_gain,
    w_router,
    routes,
    w_gate,
    w_up,
    w_down,
):
    w_out_all = lax.all_gather(w_out, CTX, axis=1, tiled=True)
    attention = attend(queries, keys, values, segment_ids)
    head_partial = jnp.dot(attention, w_out_all, preferred_element_type=F32).astype(BF)
    width = head_partial.shape[1]
    tokens = routes.shape[0]

    route_flat = routes.reshape(-1)
    expert_ids = jnp.arange(EXPERTS, dtype=jnp.int32)
    onehot = (route_flat[:, None] == expert_ids).astype(jnp.int32)
    ranks = jnp.sum((jnp.cumsum(onehot, axis=0) - onehot) * onehot, axis=-1)
    slot_of_route = (route_flat * SLOTS + ranks).reshape(tokens, 2)
    slot_ids = jnp.arange(EXPERTS * SLOTS, dtype=jnp.int32)
    hot = slot_of_route[:, :, None] == slot_ids
    picks = jnp.any(hot, axis=1).astype(BF)
    head_partial, picks, hot = lax.optimization_barrier((head_partial, picks, hot))

    head_terms = lax.all_to_all(
        head_partial.reshape(16, tokens, width), EXP, split_axis=0, concat_axis=0, tiled=True
    )
    mixed = residual.astype(F32) + jnp.sum(head_terms.astype(F32), axis=0)
    normed = (
        mixed * lax.rsqrt(jnp.mean(mixed * mixed, axis=-1, keepdims=True) + EPSILON) * norm_gain
    ).astype(BF)

    outgoing = jnp.dot(picks.T, normed, preferred_element_type=F32).astype(BF)

    incoming = lax.all_to_all(
        outgoing.reshape(EXPERTS, SLOTS, width), "z", split_axis=0, concat_axis=0, tiled=True
    ).reshape(EXPERTS * SLOTS, width)
    weights = w_gate[0], w_up[0], w_down[0]
    mine, other = plane_experts(incoming, lambda blocks: expert(blocks, *weights))
    slot_sums = scatter_plane(mine, other)
    logits = jnp.dot(normed, w_router, preferred_element_type=F32)
    chosen = jnp.sum((routes[..., None] == expert_ids).astype(F32) * logits[:, None, :], axis=-1)
    gates = jax.nn.softmax(chosen, axis=-1)
    slot_gates = jnp.sum(jnp.where(hot, gates[:, :, None], 0.0), axis=1)
    slot_sums, slot_gates = lax.optimization_barrier((slot_sums, slot_gates))
    returned = lax.all_to_all(
        slot_sums.reshape(EXPERTS, SLOTS, width), "z", split_axis=0, concat_axis=0, tiled=True
    ).reshape(EXPERTS * SLOTS, width)

    mixture = jnp.dot(
        slot_gates,
        returned.astype(F32),
        precision=lax.Precision.HIGHEST,
        preferred_element_type=F32,
    )
    return (mixed + mixture).astype(BF)


def solution(mesh):
    fine = Mesh(mesh.devices.reshape(4, 2, 2, 8, 2), ("x", "yl", "core", "z", "yh"))
    both = CTX + EXP
    placed = (
        P(CTX, EXP),
        P(CTX, None),
        P(CTX, None),
        P(CTX),
        P(both, None),
        P(EXP, CTX),
        P(),
        P(),
        P(both, None),
        P(EXP, None, CTX),
        P(EXP, None, CTX),
        P(EXP, CTX, None),
    )
    return jax.shard_map(
        shards, mesh=fine, in_specs=placed, out_specs=P(both, None), check_vma=False
    )
```
